256 devices in a mesh: txt: 8 (over z), clip: 8 (over x, core), proj: 4 (over y).
Axes of the slice: x: 4, y: 4, z: 8, core: 2. Of those that a mesh axis runs over, the one named last changes fastest.
Arguments:
- text_hidden: float32 [8192, 1024], P(('txt', 'clip')), may hold values from -16 to 16
- proj_weight: float32 [1024, 1024], P(None, 'proj'), may hold values from -2 to 2
- clip_embed: float32 [8192, 1024], P(('txt', 'clip'), 'proj'), may hold values from -16 to 16
- positive: int32 [8192], P(('txt', 'clip')), may hold values from 0 to 8191, each once
- logit_scale: float32 [1], replicated, may hold values from 10 to 300
Outputs:
- grad_hidden: float32 [8192, 1024], P(('txt', 'clip'), 'proj')
- grad_weight: float32 [1024, 1024], P(('txt', 'clip'), 'proj')
- grad_clip: float32 [8192, 1024], P(('txt', 'clip'), 'proj')
The draws below stay inside these ranges and needn't reach their ends.
Inputs may be any that keep to these rules, and one draw needn't show every extreme that they name: `positive`: each clip row is the match of exactly one text row.
All inputs are finite; a program needn't handle non-finite values.
Results may differ from the reference program's by a relative error of at most 0.0003.
Values sent between devices are 32-bit elements; how exact they have to be, the bound alone decides.
A program may use at most 64 MiB of HBM per device.

```python
import math
import jax
import jax.numpy as jnp
from jax import lax

D = 1024
ROWS = 8192


def row_field(key, salt):
    entry_key, row_key = jax.random.split(jax.random.fold_in(key, salt), 2)
    columns = 1.0 + 2.0 * jnp.arange(D, dtype=jnp.float32) / D
    rescale = jnp.exp(jax.random.uniform(row_key, (ROWS, 1), jnp.float32, math.log(0.1), 0.0))
    entries = jnp.clip(jax.random.normal(entry_key, (ROWS, D), jnp.float32), -5.0, 5.0)
    return entries * rescale * columns[None, :]


def text_base(key):
    base = row_field(key, 101)
    return base


def draw_text_hidden(key, part):
    base = text_base(key)
    return base


def draw_clip_embed(key, part):
    field = row_field(key, 202)
    return field


def draw_proj_weight(key, part):
    noise = jnp.clip(jax.random.normal(jax.random.fold_in(key, 303), (D, D), jnp.float32), -5.0, 5.0) / math.sqrt(D)
    return noise


def draw_logit_scale(key, part):
    scale_key = jax.random.fold_in(key, 404)
    return jax.random.uniform(scale_key, (1,), jnp.float32, 12.0, 30.0)


def setup_inputs(seed: int = 0) -> dict:
    key_of = jax.random.split(jax.random.key(seed), 6)
    return {
        "text_hidden": draw_text_hidden(jax.random.fold_in(key_of[5], 71), 0),
        "proj_weight": draw_proj_weight(jax.random.fold_in(key_of[5], 71), 0),
        "clip_embed": draw_clip_embed(jax.random.fold_in(key_of[5], 71), 0),
        "positive": jax.random.permutation(key_of[3], ROWS).astype(jnp.int32),
        "logit_scale": draw_logit_scale(jax.random.fold_in(key_of[5], 71), 0),
    }


EPSILON = 1e-06
PRECISE = lax.Precision.HIGHEST

def unit_rows(raw):
    inverse = lax.rsqrt(lax.optimization_barrier(jnp.sum(raw * raw, axis=1, keepdims=True)) + EPSILON)
    return (raw * inverse, inverse)

def unit_back(unit, inverse, upstream):
    along = lax.optimization_barrier(jnp.sum(unit * upstream, axis=1, keepdims=True))
    return (upstream - unit * along) * inverse

def reference(text_hidden, proj_weight, clip_embed, positive, logit_scale):
    score_scale = logit_scale[0]
    total_rows = text_hidden.shape[0]
    width = text_hidden.shape[1]
    projected = jnp.dot(text_hidden, proj_weight, precision=PRECISE, preferred_element_type=jnp.float32)
    text_unit, text_inverse = unit_rows(projected)
    clip_unit, clip_inverse = unit_rows(clip_embed)
    block_size = min(total_rows, 1024)
    block_count = total_rows // block_size
    text_blocks = text_unit.reshape(block_count, block_size, width)
    positive_blocks = positive.reshape(block_count, block_size)

    def block_scores(row_block):
        return score_scale * jnp.dot(row_block, clip_unit.T, precision=PRECISE, preferred_element_type=jnp.float32)

    def column_pass(carry, row_block):
        col_max, col_total = carry
        scores = block_scores(row_block)
        new_max = jnp.maximum(col_max, lax.optimization_barrier(jnp.max(scores, axis=0)))
        col_total = col_total * jnp.exp(col_max - new_max) + lax.optimization_barrier(jnp.sum(jnp.exp(scores - new_max[None, :]), axis=0))
        return ((new_max, col_total), None)
    start_max = jnp.full((total_rows,), -jnp.inf, jnp.float32)
    start_total = jnp.zeros((total_rows,), jnp.float32)
    (col_max, col_total), unused = lax.scan(column_pass, (start_max, start_total), text_blocks)

    def gradient_pass(clip_cot, inputs):
        row_block, positive_block = inputs
        scores = block_scores(row_block)
        row_exp = jnp.exp(scores - lax.optimization_barrier(jnp.max(scores, axis=1, keepdims=True)))
        row_prob = row_exp / lax.optimization_barrier(jnp.sum(row_exp, axis=1, keepdims=True))
        col_prob = jnp.exp(scores - col_max[None, :]) / col_total[None, :]
        matches = (lax.broadcasted_iota(jnp.int32, scores.shape, 1) == positive_block[:, None]).astype(jnp.float32)
        grad_scores = 0.5 * (row_prob + col_prob) - matches
        text_cot = score_scale * jnp.dot(grad_scores, clip_unit, precision=PRECISE, preferred_element_type=jnp.float32)
        clip_cot = clip_cot + score_scale * jnp.dot(grad_scores.T, row_block, precision=PRECISE, preferred_element_type=jnp.float32)
        return (clip_cot, text_cot)
    clip_cot, text_cots = lax.scan(gradient_pass, jnp.zeros((total_rows, width), jnp.float32), (text_blocks, positive_blocks))
    text_cot = text_cots.reshape(total_rows, width)
    text_back = unit_back(text_unit, text_inverse, text_cot)
    grad_clip = unit_back(clip_unit, clip_inverse, clip_cot)
    grad_weight = jnp.dot(text_hidden.T, text_back, precision=PRECISE, preferred_element_type=jnp.float32)
    grad_hidden = jnp.dot(text_back, proj_weight.T, precision=PRECISE, preferred_element_type=jnp.float32)
    return (grad_hidden, grad_weight, grad_clip)
```

```python
import jax
import jax.numpy as jnp
from jax import lax
from jax.experimental import pallas as pl
from jax.experimental.pallas import tpu as pltpu
from jax.sharding import PartitionSpec as P

MESH = pl.DeviceIdType.MESH
EPSILON = 1e-06
PRECISE = lax.Precision.HIGHEST
F32 = jnp.float32
BF16 = jnp.bfloat16

NAMES = {}
COUNT = 0
for _name, _n in (
    ("clip_y", 3), ("pos_x", 3), ("pos_c", 1), ("a1", 3), ("b1", 3), ("a2", 12), ("b2", 12),
    ("pa", 4), ("pb", 4), ("gz", 16), ("stat_c", 1), ("stat_y", 3), ("stat_x", 3), ("stat_z", 7),
    ("rc", 4), ("xa", 3), ("yb", 3), ("ya", 3), ("xb", 3), ("cz", 16), ("hid", 3), ("wc", 1),
    ("wx", 3), ("wz", 7), ("gc", 3),
):
    NAMES[_name] = COUNT
    COUNT += _n


def split(value):
    high = value.astype(BF16)
    return high, (value - high.astype(F32)).astype(BF16)


def product(a, b, dims):
    return lax.dot_general(a, b, (dims, ((), ())), preferred_element_type=F32)


def product3(a, b, dims):
    (ah, al), (bh, bl) = a, b
    return product(ah, bh, dims) + product(ah, bl, dims) + product(al, bh, dims)


def exact(a, b, dims):
    return lax.dot_general(a, b, (dims, ((), ())), precision=PRECISE, preferred_element_type=F32)


def turned(column):
    return jnp.broadcast_to(column, (128, 128)).T[0:1, :]


def upright(line):
    return jnp.broadcast_to(line, (128, 128)).T[:, 0:1]


def joined(stats):
    top = stats[0][0]
    for part in stats[1:]:
        top = jnp.maximum(top, part[0])
    total = stats[0][1] * jnp.exp(stats[0][0] - top)
    for part in stats[1:]:
        total = total + part[1] * jnp.exp(part[0] - top)
    return top, total


def kernel(
    hid_ref, w_ref, clip_ref, pos_ref, scale_ref,
    gh_ref, gw_ref, gc_ref,
    text, text_h, text_l, clip, clip_h, clip_l, pos, inv_t, scores, exp_r, exp_c, max_t, sum_t,
    row_stat, row_got_c, row_got_y, row_got_x, col_stat, col_got, col_keep, fac_t, g_h, g_l,
    part, part_c, got_xa, got_yb, got_ya, got_xb, cpart, cgot, hpart, hgot, wpart, wgot_c, wgot_x, wgot_z,
    cback, ss, rs,
):
    z = lax.axis_index("txt")
    k = lax.axis_index("clip")
    y = lax.axis_index("proj")
    x = k // 2
    c = lax.rem(k, 2)
    o = 1 - c

    def on_z(d):
        return lax.rem(z + d, 8)

    def on_x(d):
        return lax.rem(x + d, 4)

    def on_y(d):
        return lax.rem(y + d, 4)

    partner = (z, 2 * x + o, y)

    def z_peer(d):
        return (on_z(d), k, y)

    def x_peer(d):
        return (z, 2 * on_x(d) + c, y)

    def y_peer(d):
        return (z, k, on_y(d))

    sent = []

    def copy_of(src, dst, slot, device):
        return pltpu.make_async_remote_copy(
            src_ref=src, dst_ref=dst, send_sem=ss.at[slot], recv_sem=rs.at[slot],
            device_id=device, device_id_type=MESH,
        )

    def send(src, dst, name, at, device):
        copy = copy_of(src, dst, NAMES[name] + at, device)
        copy.start()
        sent.append(copy)

    def arrived(place, name, at):
        copy_of(place, place, NAMES[name] + at, partner).wait_recv()

    peers = [partner] + [y_peer(d) for d in (1, 2, 3)] + [x_peer(d) for d in (1, 2, 3)]
    peers += [z_peer(d) for d in range(1, 8)]
    barrier = pltpu.get_barrier_semaphore()
    for device in peers:
        pl.semaphore_signal(barrier, inc=1, device_id=device, device_id_type=MESH)
    pl.semaphore_wait(barrier, len(peers))
    scale = scale_ref[0]

    for d in (1, 2, 3):
        rows = pl.ds(pl.multiple_of(on_y(d) * 32, 32), 32)
        send(clip_ref.at[rows], clip.at[z, y], "clip_y", d - 1, y_peer(d))
    pos[c, x] = jnp.broadcast_to(pos_ref[...], (8, 128))
    for d in (1, 2, 3):
        send(pos.at[c, x], pos.at[c, x], "pos_x", d - 1, x_peer(d))
    clip[z, y] = clip_ref[pl.ds(pl.multiple_of(y * 32, 32), 32), :]

    A, B = pl.ds(0, 64), pl.ds(64, 64)
    text[y, x, c, 0:64] = exact(hid_ref[0:64, :], w_ref[...], ((1,), (0,)))
    for d in (1, 3, 2):
        send(text.at[y, x, c, A], text.at[y, x, c, A], "a1", d - 1, x_peer(d))
    text[y, x, c, 64:128] = exact(hid_ref[64:128, :], w_ref[...], ((1,), (0,)))
    for d in (1, 3, 2):
        send(text.at[y, x, c, B], text.at[y, x, c, B], "b1", d - 1, y_peer(d))

    def forward_a(e):
        block = text.at[y, on_x(4 - e), c, A]
        for d in (1, 3, 2):
            send(block, block, "a2", e * 3 + d - 1, y_peer(d))

    def forward_b(e):
        block = text.at[on_y(4 - e), x, c, B]
        for d in (1, 3, 2):
            send(block, block, "b2", e * 3 + d - 1, x_peer(d))

    def ring_clip(step):
        for h in (0, 1):
            half = pl.ds(2 * h, 2)
            for way in (0, 1):
                if step > 1:
                    ring_clip_wait(step - 1, h, way)
                if step < 4 or h == way:
                    block = clip.at[on_z(9 - step) if way == 0 else on_z(step - 1), half]
                    send(block, block, "gz", way * 8 + (step - 1) * 2 + h, z_peer(1 if way == 0 else 7))

    def ring_clip_wait(step, h, way):
        block = clip.at[on_z(8 - step) if way == 0 else on_z(step), pl.ds(2 * h, 2)]
        arrived(block, "gz", way * 8 + (step - 1) * 2 + h)

    for d in (1, 2, 3):
        arrived(clip.at[z, on_y(4 - d)], "clip_y", d - 1)
    ring_clip(1)
    forward_a(0)
    forward_b(0)
    for d in (1, 2, 3):
        arrived(pos.at[c, on_x(4 - d)], "pos_x", d - 1)
    send(pos.at[c], pos.at[c], "pos_c", 0, partner)
    for e in (1, 3, 2):
        arrived(text.at[y, on_x(4 - e), c, A], "a1", e - 1)
        forward_a(e)
        arrived(text.at[on_y(4 - e), x, c, B], "b1", e - 1)
        forward_b(e)
    ring_clip(2)
    send(text.at[y, :, c, A], text.at[y, :, c, A], "pa", 0, partner)
    send(text.at[:, x, c, B], text.at[:, x, c, B], "pb", 0, partner)
    ring_clip(3)
    ring_clip(4)
    for d in (1, 3, 2):
        for e in (0, 1, 2, 3):
            arrived(text.at[on_y(4 - d), on_x(4 - e), c, A], "a2", e * 3 + d - 1)
        group = text.at[on_y(4 - d), :, c, A]
        send(group, group, "pa", d, partner)
        for e in (0, 1, 2, 3):
            arrived(text.at[on_y(4 - e), on_x(4 - d), c, B], "b2", e * 3 + d - 1)
        group = text.at[:, on_x(4 - d), c, B]
        send(group, group, "pb", d, partner)
    ring_clip_wait(4, 0, 0)
    ring_clip_wait(4, 1, 1)

    def clip_block(f, squares):
        block = clip[:, f].reshape(256, 256)
        clip_h[f], clip_l[f] = split(block)
        return squares + jnp.sum(block * block, axis=1, keepdims=True)

    inv_c = lax.rsqrt(lax.fori_loop(0, 4, clip_block, jnp.zeros((256, 1), F32)) + EPSILON)
    col_scale = scale * inv_c

    for d in (0, 1, 3, 2):
        arrived(text.at[on_y(4 - d), :, o, A], "pa", d)
        arrived(text.at[:, on_x(4 - d), o, B], "pb", d)
    arrived(pos.at[o], "pos_c", 0)

    def score(q, carry):
        squares = jnp.zeros((256, 1), F32)
        total = jnp.zeros((256, 256), F32)
        for f in range(4):
            block = text[f, q].reshape(256, 256)
            high, low = split(block)
            text_h[f, q], text_l[f, q] = high, low
            squares = squares + jnp.sum(block * block, axis=1, keepdims=True)
            total = total + product3((clip_h[f], clip_l[f]), (high, low), ((1,), (1,)))
        inverse = lax.rsqrt(squares + EPSILON)
        lanes = jnp.concatenate([turned(inverse[0:128]), turned(inverse[128:256])], axis=1)
        inv_t[q] = jnp.broadcast_to(lanes, (8, 256))
        tile = total * col_scale * lanes
        scores[q] = tile
        top = jnp.max(tile, axis=0, keepdims=True)
        raised = jnp.exp(tile - top)
        exp_r[q] = raised
        max_t[q] = jnp.broadcast_to(top, (8, 256))
        sum_t[q] = jnp.broadcast_to(jnp.sum(raised, axis=0, keepdims=True), (8, 256))
        return carry

    lax.fori_loop(0, 4, score, 0)

    for q in range(4):
        for h in (0, 1):
            row = 2 * q + h
            row_stat[0, row : row + 1, :] = max_t[q, 0:1, h * 128 : h * 128 + 128]
            row_stat[0, 8 + row : 9 + row, :] = sum_t[q, 0:1, h * 128 : h * 128 + 128]
    send(row_stat.at[0], row_got_c, "stat_c", 0, partner)
    top_c = jnp.max(scores[0], axis=1, keepdims=True)
    for q in range(1, 4):
        top_c = jnp.maximum(top_c, jnp.max(scores[q], axis=1, keepdims=True))
    total_c = jnp.zeros((256, 1), F32)
    for q in range(4):
        raised = jnp.exp(scores[q] - top_c)
        exp_c[q] = raised
        total_c = total_c + jnp.sum(raised, axis=1, keepdims=True)
    for h in (0, 1):
        col_stat[h : h + 1, :] = turned(top_c[h * 128 : h * 128 + 128])
        col_stat[2 + h : 3 + h, :] = turned(total_c[h * 128 : h * 128 + 128])
    col_stat[4:8, :] = jnp.zeros((4, 128), F32)
    for d in range(1, 8):
        send(col_stat, col_got.at[d - 1], "stat_z", d - 1, z_peer(d))

    def row_part(value):
        return value[0:8], value[8:16]

    arrived(row_got_c, "stat_c", 0)
    stats = joined([row_part(row_stat[0]), row_part(row_got_c[...])])
    row_stat[1, 0:8], row_stat[1, 8:16] = stats
    for d in (1, 3, 2):
        send(row_stat.at[1], row_got_y.at[d - 1], "stat_y", d - 1, y_peer(d))
    for d in (1, 2, 3):
        arrived(row_got_y.at[d - 1], "stat_y", d - 1)
    stats = joined([stats] + [row_part(row_got_y[d]) for d in range(3)])
    row_stat[2, 0:8], row_stat[2, 8:16] = stats
    for d in (1, 3, 2):
        send(row_stat.at[2], row_got_x.at[d - 1], "stat_x", d - 1, x_peer(d))
    for d in range(1, 8):
        arrived(col_got.at[d - 1], "stat_z", d - 1)

    def col_part(value):
        return value[0:2], value[2:4]

    top_g, total_g = joined([col_part(col_stat[...])] + [col_part(col_got[d]) for d in range(7)])
    fac = 0.5 * jnp.exp(col_stat[0:2] - top_g) / total_g
    fac_c = jnp.concatenate([upright(fac[0:1]), upright(fac[1:2])], axis=0)
    for d in (1, 2, 3):
        arrived(row_got_x.at[d - 1], "stat_x", d - 1)
    top_g, total_g = joined([stats] + [row_part(row_got_x[d]) for d in range(3)])
    fac = 0.5 * jnp.exp(row_stat[0, 0:8] - top_g) / total_g
    for q in range(4):
        for h in (0, 1):
            row = 2 * q + h
            fac_t[q, :, h * 128 : h * 128 + 128] = jnp.broadcast_to(fac[row : row + 1], (8, 128))

    number = lax.broadcasted_iota(jnp.int32, (256, 256), 0)
    clip_id = lax.shift_right_logical(number, 5) * 1024 + (number & 31) + (k * 128 + y * 32)

    def gradient(q, carry):
        target = jnp.concatenate([pos[0, q, 0:1, :], pos[1, q, 0:1, :]], axis=1)
        grad = exp_r[q] * fac_t[q, 0:1, :] + exp_c[q] * fac_c
        grad = grad - (clip_id == target).astype(F32)
        along = jnp.sum(grad * scores[q], axis=0, keepdims=True)
        g_h[q], g_l[q] = split(grad * (scale * inv_t[q, 0:1, :]))
        weighted = split(grad * col_scale)
        for f in range(4):
            block = product3(weighted, (clip_h[f], clip_l[f]), ((0,), (0,)))
            part[f, q, :, 8:136] = block.reshape(2, 128, 256)
            for h in (0, 1):
                line = jnp.broadcast_to(along[:, h * 128 : h * 128 + 128], (8, 128))
                part[f, q, h, 0:8] = jnp.concatenate([line, line], axis=1)
        copy_of(part.at[:, q, o], part_c.at[:, q], NAMES["rc"] + q, partner).start()
        return carry

    lax.fori_loop(0, 4, gradient, 0)
    for q in range(4):
        sent.append(copy_of(part.at[:, q, o], part_c.at[:, q], NAMES["rc"] + q, partner))

    def clip_gradient(f, carry):
        total = jnp.zeros((256, 256), F32)
        for q in range(4):
            total = total + product3((g_h[q], g_l[q]), (text_h[f, q], text_l[f, q]), ((1,), (0,)))
        cpart[:, f] = total.reshape(8, 32, 256)
        return carry

    lax.fori_loop(0, 4, clip_gradient, 0)

    def ring_sum(step):
        for h in (0, 1):
            half = pl.ds(2 * h, 2)
            for way in (0, 1):
                goal = on_z(5 - step) if way == 0 else on_z(3 + step)
                if step > 2 or (step == 2 and h == way):
                    place = cgot.at[way, step - 2, h]
                    arrived(place, "cz", way * 8 + (step - 2) * 2 + h)
                    cpart[goal, half] = cpart[goal, half] + place[...]
                if step > 1 or h == way:
                    send(
                        cpart.at[goal, half], cgot.at[way, step - 1, h],
                        "cz", way * 8 + (step - 1) * 2 + h, z_peer(1 if way == 0 else 7),
                    )

    ring_sum(1)
    for q in range(4):
        arrived(part_c.at[:, q], "rc", q)

    def add_core(q, carry):
        for f in range(4):
            part[f, q, c] = part[f, q, c] + part_c[f, q]
        return carry

    lax.fori_loop(0, 4, add_core, 0)
    first, second = pl.ds(0, 72), pl.ds(72, 64)
    for d in (1, 3, 2):
        send(part.at[:, on_x(d), c, first], got_xa.at[d - 1], "xa", d - 1, x_peer(d))
        send(part.at[on_y(d), :, c, second], got_yb.at[d - 1], "yb", d - 1, y_peer(d))
    ring_sum(2)
    ring_sum(3)
    ring_sum(4)
    for d in (1, 3, 2):
        arrived(got_xa.at[d - 1], "xa", d - 1)
        arrived(got_yb.at[d - 1], "yb", d - 1)

    def add_first(e, carry):
        part[e, x, c, 0:72] = part[e, x, c, 0:72] + got_xa[0, e] + got_xa[1, e] + got_xa[2, e]
        part[y, e, c, 72:136] = part[y, e, c, 72:136] + got_yb[0, e] + got_yb[1, e] + got_yb[2, e]
        return carry

    lax.fori_loop(0, 4, add_first, 0)
    for d in (1, 3, 2):
        send(part.at[on_y(d), x, c, first], got_ya.at[d - 1], "ya", d - 1, y_peer(d))
        send(part.at[y, on_x(d), c, second], got_xb.at[d - 1], "xb", d - 1, x_peer(d))

    for way in (0, 1):
        for h in (0, 1):
            arrived(cgot.at[way, 3, h], "cz", way * 8 + 6 + h)
    squares = jnp.zeros((32, 1), F32)
    along = jnp.zeros((32, 1), F32)
    for f in range(4):
        total = cpart[z, f] + cgot[0, 3, f // 2, f % 2] + cgot[1, 3, f // 2, f % 2]
        raw = clip[z, f]
        cback[f] = total
        squares = squares + jnp.sum(raw * raw, axis=1, keepdims=True)
        along = along + jnp.sum(raw * total, axis=1, keepdims=True)
    inverse = lax.rsqrt(squares + EPSILON)
    for f in range(4):
        cback[f] = (cback[f] - (clip[z, f] * inverse) * (along * inverse)) * inverse
    for d in (1, 3, 2):
        send(cback.at[on_y(d)], col_keep.at[d - 1], "gc", d - 1, y_peer(d))

    squares = jnp.zeros((128, 1), F32)
    for f in range(4):
        raw = text[f, x, c]
        squares = squares + jnp.sum(raw * raw, axis=1, keepdims=True)
    inverse = lax.rsqrt(squares + EPSILON)
    for d in (1, 3, 2):
        arrived(got_ya.at[d - 1], "ya", d - 1)
        arrived(got_xb.at[d - 1], "xb", d - 1)
    upper = part[y, x, c, 0:72] + got_ya[0] + got_ya[1] + got_ya[2]
    lower = part[y, x, c, 72:136] + got_xb[0] + got_xb[1] + got_xb[2]
    along = upright(upper[0:1, 0:128])
    cot = jnp.concatenate([upper[8:72], lower], axis=0)
    back = (cot - (text[y, x, c] * inverse) * along) * inverse

    for e in range(4):
        rows = slice(256 * e, 256 * e + 256)
        block = exact(hid_ref[:, rows], back, ((0,), (0,)))
        wpart[2 * e : 2 * e + 2] = block.reshape(2, 4, 2, 16, 256)
    send(wpart.at[:, :, o], wgot_c, "wc", 0, partner)
    for d in (2, 1, 3):
        rows = pl.ds(pl.multiple_of(on_y(d) * 256, 256), 256)
        hpart[d] = exact(back, w_ref[rows, :], ((1,), (1,)))
        send(hpart.at[d], hgot.at[d - 1], "hid", d - 1, y_peer(d))
    arrived(wgot_c, "wc", 0)

    def add_weight(e, carry):
        for f in range(4):
            wpart[e, f, c] = wpart[e, f, c] + wgot_c[e, f]
        return carry

    lax.fori_loop(0, 8, add_weight, 0)
    for d in (2, 1, 3):
        send(wpart.at[:, on_x(d), c], wgot_x.at[d - 1], "wx", d - 1, x_peer(d))
    own = exact(back, w_ref[pl.ds(pl.multiple_of(y * 256, 256), 256), :], ((1,), (1,)))
    for d in (1, 3, 2):
        arrived(wgot_x.at[d - 1], "wx", d - 1)
    wpart[:, x, c] = wpart[:, x, c] + wgot_x[0] + wgot_x[1] + wgot_x[2]
    for d in (4, 3, 5, 2, 6, 1, 7):
        send(wpart.at[on_z(d), x, c], wgot_z.at[d - 1], "wz", d - 1, z_peer(d))
    gc_ref[pl.ds(pl.multiple_of(y * 32, 32), 32), :] = cback[y]
    for d in (1, 2, 3):
        arrived(col_keep.at[d - 1], "gc", d - 1)
        gc_ref[pl.ds(pl.multiple_of(on_y(4 - d) * 32, 32), 32), :] = col_keep[d - 1]
    for d in (1, 3, 2):
        arrived(hgot.at[d - 1], "hid", d - 1)
    gh_ref[...] = own + hgot[0] + hgot[1] + hgot[2]
    total = wpart[z, x, c]
    for d in (1, 7, 2, 6, 3, 5, 4):
        arrived(wgot_z.at[d - 1], "wz", d - 1)
        total = total + wgot_z[d - 1]
    gw_ref[...] = total
    for copy in sent:
        copy.wait_send()


def body(text_hidden, proj_weight, clip_embed, positive, logit_scale):
    vmem = pl.BlockSpec(memory_space=pltpu.VMEM)
    scratch = [
        ((4, 4, 2, 128, 256), F32), ((4, 4, 256, 256), BF16), ((4, 4, 256, 256), BF16),
        ((8, 4, 32, 256), F32), ((4, 256, 256), BF16), ((4, 256, 256), BF16),
        ((2, 4, 8, 128), jnp.int32), ((4, 8, 256), F32),
        ((4, 256, 256), F32), ((4, 256, 256), F32), ((4, 256, 256), F32), ((4, 8, 256), F32), ((4, 8, 256), F32),
        ((3, 16, 128), F32), ((16, 128), F32), ((3, 16, 128), F32), ((3, 16, 128), F32),
        ((8, 128), F32), ((7, 8, 128), F32), ((3, 32, 256), F32), ((4, 8, 256), F32),
        ((4, 256, 256), BF16), ((4, 256, 256), BF16),
        ((4, 4, 2, 136, 256), F32), ((4, 4, 136, 256), F32),
        ((3, 4, 72, 256), F32), ((3, 4, 64, 256), F32), ((3, 72, 256), F32), ((3, 64, 256), F32),
        ((8, 4, 32, 256), F32), ((2, 4, 2, 2, 32, 256), F32),
        ((4, 128, 256), F32), ((3, 128, 256), F32),
        ((8, 4, 2, 16, 256), F32), ((8, 4, 16, 256), F32), ((3, 8, 16, 256), F32), ((7, 16, 256), F32),
        ((4, 32, 256), F32),
    ]
    return pl.pallas_call(
        kernel,
        out_shape=(
            jax.ShapeDtypeStruct((128, 256), F32),
            jax.ShapeDtypeStruct((16, 256), F32),
            jax.ShapeDtypeStruct((128, 256), F32),
        ),
        in_specs=[vmem, vmem, vmem, vmem, pl.BlockSpec(memory_space=pltpu.SMEM)],
        out_specs=(vmem, vmem, vmem),
        scratch_shapes=[pltpu.VMEM(shape, dtype) for shape, dtype in scratch]
        + [pltpu.SemaphoreType.DMA((COUNT,)), pltpu.SemaphoreType.DMA((COUNT,))],
        compiler_params=pltpu.CompilerParams(
            collective_id=0, has_side_effects=True, vmem_limit_bytes=56 << 20
        ),
        name="contrastive",
    )(text_hidden, proj_weight, clip_embed, positive.reshape(1, 128), logit_scale)


def solution(mesh):
    rows = ("txt", "clip")
    in_specs = (P(rows, None), P(None, "proj"), P(rows, "proj"), P(rows), P())
    out_specs = (P(rows, "proj"), P(rows, "proj"), P(rows, "proj"))
    return jax.shard_map(body, mesh=mesh, in_specs=in_specs, out_specs=out_specs, check_vma=False)
```

```python
import math

import jax
import jax.numpy as jnp
from jax import lax
from jax.experimental import pallas as pl
from jax.experimental.pallas import tpu as pltpu
from jax.sharding import PartitionSpec as P

MESH = pl.DeviceIdType.MESH
EPSILON = 1e-06
PRECISE = lax.Precision.HIGHEST
F32 = jnp.float32
BF16 = jnp.bfloat16

COUNT = 136
GROUPS = 8
GROUP_TILES = 1024
TURN = (1, 3)
CAME = (3, 1)
CHUNKS = (2, 1, 3, 0)


def split(value):
    high = value.astype(BF16)
    return high, (value - high.astype(F32)).astype(BF16)


def product(a, b, dims):
    return lax.dot_general(a, b, (dims, ((), ())), preferred_element_type=F32)


def product3(a, b, dims):
    (ah, al), (bh, bl) = a, b
    return product(ah, bh, dims) + product(ah, bl, dims) + product(al, bh, dims)


def exact(a, b, dims):
    return lax.dot_general(a, b, (dims, ((), ())), precision=PRECISE, preferred_element_type=F32)


def turned(column):
    return jnp.broadcast_to(column, (128, 128)).T[0:1, :]


def upright(line):
    return jnp.broadcast_to(line, (128, 128)).T[:, 0:1]


def joined(stats):
    top = stats[0][0]
    for part in stats[1:]:
        top = jnp.maximum(top, part[0])
    total = stats[0][1] * jnp.exp(stats[0][0] - top)
    for part in stats[1:]:
        total = total + part[1] * jnp.exp(part[0] - top)
    return top, total


def kernel(
    hid_hbm, w_hbm, clip_ref, pos_ref, scale_ref,
    gh_ref, gw_ref, gc_ref,
    text, text_h, text_l, clip, clip_h, clip_l, pos, inv_t, scores, exp_r, exp_c, max_t, sum_t,
    row_stat, row_got_y, row_got_x, col_stat, col_got, col_keep, fac_t, g_h, g_l,
    part, part_c, got_aa, got_bb, got_a, got_b, got_ya, got_xb,
    along_own, along_c, along_pair, along_y, along_sum, along_x, cpart, cgot, hpart, hgot, wpart, wgot_c, wgot_x, wgot_z,
    cback, hid_ref, w_ref, blank, ss, rs, ls,
):
    z = lax.axis_index("txt")
    k = lax.axis_index("clip")
    y = lax.axis_index("proj")
    x = k // 2
    c = lax.rem(k, 2)
    o = 1 - c

    def on_z(d):
        return lax.rem(z + d, 8)

    def on_x(d):
        return lax.rem(x + d, 4)

    def on_y(d):
        return lax.rem(y + d, 4)

    partner = (z, 2 * x + o, y)

    def z_peer(d):
        return (on_z(d), k, y)

    def x_peer(d):
        return (z, 2 * on_x(d) + c, y)

    def y_peer(d):
        return (z, k, on_y(d))

    def y_other(d):
        return (z, 2 * x + o, on_y(d))

    groups = [0]
    places = {}

    def slot(key):
        return places.setdefault(key, len(places))

    def copy_of(src, dst, key, device):
        return pltpu.make_async_remote_copy(
            src_ref=src, dst_ref=dst, send_sem=ss.at[len(groups) - 1], recv_sem=rs.at[slot(key)],
            device_id=device, device_id_type=MESH,
        )

    def send(src, dst, key, device):
        tiles = math.prod(src.shape) // 1024
        if groups[-1] + tiles > GROUP_TILES:
            groups.append(0)
        groups[-1] += tiles
        copy_of(src, dst, key, device).start()

    def arrived(place, key):
        copy_of(place, place, key, partner).wait_recv()

    peers = [partner] + [y_peer(d) for d in (1, 2, 3)] + [x_peer(d) for d in (1, 2, 3)]
    peers += [z_peer(d) for d in range(1, 8)] + [y_other(d) for d in (1, 2, 3)]
    barrier = pltpu.get_barrier_semaphore()
    for device in peers:
        pl.semaphore_signal(barrier, inc=1, device_id=device, device_id_type=MESH)
    loads = [
        pltpu.make_async_copy(hid_hbm, hid_ref, ls.at[0]),
        pltpu.make_async_copy(w_hbm, w_ref, ls.at[1]),
    ]
    for load in loads:
        load.start()
    scale = scale_ref[0]
    pos[c, x] = jnp.broadcast_to(pos_ref[...], (8, 128))
    clip[z, y] = clip_ref[pl.ds(pl.multiple_of(y * 32, 32), 32), :]
    for load in loads:
        load.wait()
    text[y, x, c] = exact(hid_ref[...], w_ref[...], ((1,), (0,)))
    pl.semaphore_wait(barrier, len(peers))

    for d in (1, 2, 3):
        rows = pl.ds(pl.multiple_of(on_y(d) * 32, 32), 32)
        send(clip_ref.at[rows], clip.at[z, y], ("clip_y", d), y_peer(d))
    for d in (1, 2, 3):
        send(pos.at[c, x], pos.at[c, x], ("pos_x", d - 1), x_peer(d))

    def rows_of(kind, part=None):
        return pl.ds(64 * kind, 64) if part is None else pl.ds(64 * kind + 32 * part, 32)

    def block_of(kind, near, far, part=None):
        dy, dx = (far, near) if kind == 0 else (near, far)
        return text.at[on_y(dy), on_x(dx), c, rows_of(kind, part)]

    def near_peer(kind, d):
        return x_peer(d) if kind == 0 else y_peer(d)

    def far_peer(kind, d):
        return y_peer(d) if kind == 0 else x_peer(d)

    def spread(block, key, device):
        send(block, block, key, device)

    def begin(kind):
        for way in (0, 1):
            spread(block_of(kind, 0, 0), ("n", kind, way), near_peer(kind, TURN[way]))

    def cross(kind, e):
        for way in (0, 1):
            spread(block_of(kind, e, 0), ("f", kind, e, way), far_peer(kind, TURN[way]))

    def relay_near(kind):
        for way in (0, 1):
            arrived(block_of(kind, CAME[way], 0), ("n", kind, way))
            spread(block_of(kind, CAME[way], 0, way), ("nn", kind), near_peer(kind, TURN[way]))

    def relay_far(kind, e):
        for way in (0, 1):
            arrived(block_of(kind, e, CAME[way]), ("f", kind, e, way))
            spread(block_of(kind, e, CAME[way], way), ("ff", kind), far_peer(kind, TURN[way]))

    def group_of(kind, far, core):
        rows = rows_of(kind)
        return text.at[on_y(far), :, core, rows] if kind == 0 else text.at[:, on_x(far), core, rows]

    def to_partner(kind, far):
        spread(group_of(kind, far, c), ("p", kind, far), partner)

    def clip_piece(far, d):
        return clip.at[on_z(far), on_y(d)]

    def ring_clip(step, d):
        for way in (0, 1):
            if step > 1:
                ring_clip_wait(step - 1, d, way)
            if step < 4 or d in ((0, 3), (1, 2))[way]:
                block = clip_piece(9 - step if way == 0 else step - 1, d)
                spread(block, ("gz", step, d, way), z_peer(1 if way == 0 else 7))

    def ring_clip_wait(step, d, way):
        arrived(clip_piece(8 - step if way == 0 else step, d), ("gz", step, d, way))

    ring_clip(1, 0)
    for kind in (0, 1):
        begin(kind)
    for kind in (0, 1):
        cross(kind, 0)
    for d in (1, 3, 2):
        arrived(clip_piece(0, d), ("clip_y", 4 - d))
        ring_clip(1, d)
    for d in (1, 2, 3):
        arrived(pos.at[c, on_x(4 - d)], ("pos_x", d - 1))
    send(pos.at[c], pos.at[c], ("pos_c", 0), partner)
    ring_clip(2, 0)
    for kind in (0, 1):
        relay_near(kind)
        for e in CAME:
            cross(kind, e)
    for d in (1, 3, 2):
        ring_clip(2, d)
    for kind in (0, 1):
        relay_far(kind, 0)
    ring_clip(3, 0)
    for kind in (0, 1):
        arrived(block_of(kind, 2, 0), ("nn", kind))
        cross(kind, 2)
    for d in (1, 3, 2):
        ring_clip(3, d)
    for kind in (0, 1):
        to_partner(kind, 0)
        for e in CAME:
            relay_far(kind, e)
    ring_clip(4, 0)
    for d in (1, 3, 2):
        ring_clip(4, d)
    for kind in (0, 1):
        relay_far(kind, 2)
        for d in CAME:
            to_partner(kind, d)
    for kind in (0, 1):
        arrived(group_of(kind, 2, c), ("ff", kind))
        to_partner(kind, 2)
    for d in (0, 1, 3, 2):
        ring_clip_wait(4, d, 0 if d in (0, 3) else 1)

    def clip_block(f, squares):
        block = clip[:, f].reshape(256, 256)
        clip_h[f], clip_l[f] = split(block)
        return squares + jnp.sum(block * block, axis=1, keepdims=True)

    inv_c = lax.rsqrt(lax.fori_loop(0, 4, clip_block, jnp.zeros((256, 1), F32)) + EPSILON)
    col_scale = scale * inv_c

    for d in (0, 1, 3, 2):
        for kind in (0, 1):
            arrived(group_of(kind, d, o), ("p", kind, d))
    arrived(pos.at[o], ("pos_c", 0))

    def score(q, carry):
        squares = jnp.zeros((256, 1), F32)
        total = jnp.zeros((256, 256), F32)
        for f in range(4):
            block = text[f, q].reshape(256, 256)
            high, low = split(block)
            text_h[f, q], text_l[f, q] = high, low
            squares = squares + jnp.sum(block * block, axis=1, keepdims=True)
            total = total + product3((clip_h[f], clip_l[f]), (high, low), ((1,), (1,)))
        inverse = lax.rsqrt(squares + EPSILON)
        lanes = jnp.concatenate([turned(inverse[0:128]), turned(inverse[128:256])], axis=1)
        inv_t[q] = jnp.broadcast_to(lanes, (8, 256))
        tile = total * col_scale * lanes
        scores[q] = tile
        top = jnp.max(tile, axis=0, keepdims=True)
        raised = jnp.exp(tile - top)
        exp_r[q] = raised
        max_t[q] = jnp.broadcast_to(top, (8, 256))
        sum_t[q] = jnp.broadcast_to(jnp.sum(raised, axis=0, keepdims=True), (8, 256))
        return carry

    lax.fori_loop(0, 4, score, 0)

    for q in range(4):
        for h in (0, 1):
            row = 2 * q + h
            row_stat[0, row : row + 1, :] = max_t[q, 0:1, h * 128 : h * 128 + 128]
            row_stat[0, 8 + row : 9 + row, :] = sum_t[q, 0:1, h * 128 : h * 128 + 128]
    send(row_stat.at[0], row_got_y.at[0], ("stat",), partner)
    for d in (2, 1, 3):
        send(row_stat.at[0], row_got_y.at[d], ("stat",), y_peer(d))
        send(row_stat.at[0], row_got_y.at[3 + d], ("stat",), y_other(d))
    top_c = jnp.max(scores[0], axis=1, keepdims=True)
    for q in range(1, 4):
        top_c = jnp.maximum(top_c, jnp.max(scores[q], axis=1, keepdims=True))
    total_c = jnp.zeros((256, 1), F32)
    for q in range(4):
        raised = jnp.exp(scores[q] - top_c)
        exp_c[q] = raised
        total_c = total_c + jnp.sum(raised, axis=1, keepdims=True)
    for h in (0, 1):
        col_stat[h : h + 1, :] = turned(top_c[h * 128 : h * 128 + 128])
        col_stat[2 + h : 3 + h, :] = turned(total_c[h * 128 : h * 128 + 128])
    col_stat[4:8, :] = jnp.zeros((4, 128), F32)
    for d in range(1, 8):
        send(col_stat, col_got.at[d - 1], ("stat_z",), z_peer(d))

    def row_part(value):
        return value[0:8], value[8:16]

    arrived(row_got_y, ("stat",))
    stats = joined([row_part(row_stat[0])] + [row_part(row_got_y[d]) for d in range(7)])
    row_stat[2, 0:8], row_stat[2, 8:16] = stats
    for d in (1, 3, 2):
        send(row_stat.at[2], row_got_x.at[d - 1], ("stat_x",), x_peer(d))
    arrived(col_got, ("stat_z",))

    def col_part(value):
        return value[0:2], value[2:4]

    top_g, total_g = joined([col_part(col_stat[...])] + [col_part(col_got[d]) for d in range(7)])
    fac = 0.5 * jnp.exp(col_stat[0:2] - top_g) / total_g
    fac_c = jnp.concatenate([upright(fac[0:1]), upright(fac[1:2])], axis=0)
    arrived(row_got_x, ("stat_x",))
    top_g, total_g = joined([stats] + [row_part(row_got_x[d]) for d in range(3)])
    fac = 0.5 * jnp.exp(row_stat[0, 0:8] - top_g) / total_g
    for q in range(4):
        for h in (0, 1):
            row = 2 * q + h
            fac_t[q, :, h * 128 : h * 128 + 128] = jnp.broadcast_to(fac[row : row + 1], (8, 128))

    number = lax.broadcasted_iota(jnp.int32, (256, 256), 0)
    clip_id = lax.shift_right_logical(number, 5) * 1024 + (number & 31) + (k * 128 + y * 32)

    def gradient(i):
        q = on_x(CHUNKS[i])
        target = jnp.concatenate([pos[0, q, 0:1, :], pos[1, q, 0:1, :]], axis=1)
        grad = exp_r[q] * fac_t[q, 0:1, :] + exp_c[q] * fac_c
        grad = grad - (clip_id == target).astype(F32)
        line = jnp.sum(grad * scores[q], axis=0, keepdims=True)
        for h in (0, 1):
            along_own[2 * i + h : 2 * i + h + 1, :] = line[:, h * 128 : h * 128 + 128]
        g_h[q], g_l[q] = split(grad * (scale * inv_t[q, 0:1, :]))
        weighted = split(grad * col_scale)
        for f in range(4):
            block = product3(weighted, (clip_h[f], clip_l[f]), ((0,), (0,)))
            part[f, q] = block.reshape(2, 128, 256)
        send(part.at[:, q, o], part_c.at[:, q], ("rc", i), partner)

    for i in range(4):
        gradient(i)
    send(along_own, along_c, ("along_c", 0), partner)

    def clip_gradient(f, carry):
        total = jnp.zeros((256, 256), F32)
        for q in range(4):
            total = total + product3((g_h[q], g_l[q]), (text_h[f, q], text_l[f, q]), ((1,), (0,)))
        cpart[:, f] = total.reshape(8, 32, 256)
        return carry

    lax.fori_loop(0, 4, clip_gradient, 0)

    def ring_sum(step):
        for f in range(4):
            for way in (0, 1):
                goal = on_z(5 - step) if way == 0 else on_z(3 + step)
                if step > 2 or (step == 2 and f // 2 == way):
                    place = cgot.at[way, step - 2, f]
                    arrived(place, ("cz", step - 1, f, way))
                    cpart[goal, f] = cpart[goal, f] + place[...]
                if step > 1 or f // 2 == way:
                    send(
                        cpart.at[goal, f], cgot.at[way, step - 1, f],
                        ("cz", step, f if step < 4 else 0, way), z_peer(1 if way == 0 else 7),
                    )

    def half_of(part):
        return pl.ds(32 * part, 32)

    def pass_a(d, way, half):
        send(
            part.at[:, on_x(d), c, rows_of(0, half)], got_a.at[way, :, half_of(half)],
            ("ra", way), x_peer(TURN[way]),
        )

    def pass_b(i, d, way, half):
        send(
            part.at[on_y(d), on_x(CHUNKS[i]), c, rows_of(1, half)], got_b.at[way, i, half_of(half)],
            ("rb", i, way), y_peer(TURN[way]),
        )

    def join_cores(i):
        q = on_x(CHUNKS[i])
        arrived(part_c.at[:, q], ("rc", i))
        for f in range(4):
            part[f, q, c] = part[f, q, c] + part_c[f, q]
        for way in (0, 1):
            if i == 0:
                send(
                    part.at[:, q, c, rows_of(0, way)], got_aa.at[way], ("raa", way), x_peer(TURN[way])
                )
            if CHUNKS[i] == TURN[way]:
                pass_a(TURN[way], way, 1 - way)
            send(
                part.at[on_y(2), q, c, rows_of(1, way)], got_bb.at[way, i], ("rbb", i, way),
                y_peer(TURN[way]),
            )
        for way in (0, 1):
            pass_b(i, TURN[way], way, 1 - way)

    def relay_a():
        for way in (0, 1):
            arrived(got_aa.at[way], ("raa", way))
            at = slice(32 * way, 32 * way + 32)
            for f in range(4):
                part[f, on_x(TURN[way]), c, at] = part[f, on_x(TURN[way]), c, at] + got_aa[way, f]
            pass_a(TURN[way], way, way)

    def relay_b(i):
        q = on_x(CHUNKS[i])
        for way in (0, 1):
            arrived(got_bb.at[way, i], ("rbb", i, way))
            at = slice(64 + 32 * way, 96 + 32 * way)
            part[on_y(TURN[way]), q, c, at] = part[on_y(TURN[way]), q, c, at] + got_bb[way, i]
            pass_b(i, TURN[way], way, way)

    def finish_a():
        for way in (0, 1):
            arrived(got_a.at[way], ("ra", way))
        for d in (2, 1, 3, 0):
            e = on_y(d)
            part[e, x, c, 0:64] = part[e, x, c, 0:64] + got_a[0, e] + got_a[1, e]
            if d > 0:
                send(part.at[e, x, c, rows_of(0)], got_ya.at[d - 1], ("ya",), y_peer(d))

    def finish_b(i):
        q = on_x(CHUNKS[i])
        for way in (0, 1):
            arrived(got_b.at[way, i], ("rb", i, way))
        part[y, q, c, 64:128] = part[y, q, c, 64:128] + got_b[0, i] + got_b[1, i]
        d = CHUNKS[i]
        if d > 0:
            send(part.at[y, q, c, rows_of(1)], got_xb.at[d - 1], ("xb",), x_peer(d))

    join_cores(0)
    ring_sum(1)
    join_cores(1)
    join_cores(2)
    join_cores(3)
    arrived(along_c, ("along_c", 0))
    along_pair[...] = along_own[...] + along_c[...]
    for d in (2, 1, 3):
        send(along_pair, along_y.at[d - 1], ("along_y",), y_peer(d))
    relay_a()
    relay_b(0)
    ring_sum(2)
    relay_b(1)
    relay_b(2)
    arrived(along_y, ("along_y",))
    along_sum[...] = along_pair[...] + along_y[0] + along_y[1] + along_y[2]
    for d in (2, 1, 3):
        send(along_sum, along_x.at[d - 1], ("along_x",), x_peer(d))
    relay_b(3)
    ring_sum(3)
    finish_b(0)
    finish_a()
    for i in (1, 2, 3):
        finish_b(i)
    ring_sum(4)

    for way in (0, 1):
        arrived(cgot.at[way, 3], ("cz", 4, 0, way))
    squares = jnp.zeros((32, 1), F32)
    along = jnp.zeros((32, 1), F32)
    for f in range(4):
        total = cpart[z, f] + cgot[0, 3, f] + cgot[1, 3, f]
        raw = clip[z, f]
        cback[f] = total
        squares = squares + jnp.sum(raw * raw, axis=1, keepdims=True)
        along = along + jnp.sum(raw * total, axis=1, keepdims=True)
    inverse = lax.rsqrt(squares + EPSILON)
    for f in range(4):
        cback[f] = (cback[f] - (clip[z, f] * inverse) * (along * inverse)) * inverse
    for d in (1, 3, 2):
        send(cback.at[on_y(d)], col_keep.at[d - 1], ("gc",), y_peer(d))

    squares = jnp.zeros((128, 1), F32)
    for f in range(4):
        raw = text[f, x, c]
        squares = squares + jnp.sum(raw * raw, axis=1, keepdims=True)
    inverse = lax.rsqrt(squares + EPSILON)
    arrived(got_ya, ("ya",))
    arrived(got_xb, ("xb",))
    arrived(along_x, ("along_x",))
    lines = along_sum[6:8]
    for d in (1, 2, 3):
        at = 2 * CHUNKS.index(d)
        lines = lines + along_x[d - 1, at : at + 2]
    along = upright(jnp.where(c == 0, lines[0:1], lines[1:2]))
    upper = part[y, x, c, 0:64] + got_ya[0] + got_ya[1] + got_ya[2]
    lower = part[y, x, c, 64:128] + got_xb[0] + got_xb[1] + got_xb[2]
    cot = jnp.concatenate([upper, lower], axis=0)
    back = (cot - (text[y, x, c] * inverse) * along) * inverse

    order = (4, 3, 5, 2, 6, 1, 7, 0)

    def weight(t):
        for j in range(4 * t, 4 * t + 4):
            rows = pl.ds(pl.multiple_of(on_z(order[j]) * 128, 128), 128)
            wpart[j] = exact(hid_ref[:, rows], back, ((0,), (0,))).reshape(4, 2, 16, 256)
        send(wpart.at[4 * t : 4 * t + 4, :, o], wgot_c.at[4 * t : 4 * t + 4], ("wc", t), partner)

    def hidden(d):
        rows = pl.ds(pl.multiple_of(on_y(d) * 256, 256), 256)
        hpart[d] = exact(back, w_ref[rows, :], ((1,), (1,)))
        if d > 0:
            send(hpart.at[d], hgot.at[d - 1], ("hid",), y_peer(d))

    def weight_x(t):
        arrived(wgot_c.at[4 * t : 4 * t + 4], ("wc", t))
        for j in range(4 * t, 4 * t + 4):
            for f in range(4):
                wpart[j, f, c] = wpart[j, f, c] + wgot_c[j, f]
        for d in (2, 1, 3):
            send(
                wpart.at[4 * t : 4 * t + 4, on_x(d), c], wgot_x.at[d - 1, 4 * t : 4 * t + 4],
                ("wx", t), x_peer(d),
            )

    def weight_z(t):
        arrived(wgot_x.at[:, 4 * t : 4 * t + 4], ("wx", t))
        for j in range(4 * t, 4 * t + 4):
            wpart[j, x, c] = wpart[j, x, c] + wgot_x[0, j] + wgot_x[1, j] + wgot_x[2, j]
            d = order[j]
            if d > 0:
                send(wpart.at[j, x, c], wgot_z.at[d - 1], ("wz",), z_peer(d))

    weight(0)
    hidden(2)
    weight(1)
    weight_x(0)
    hidden(1)
    hidden(3)
    weight_x(1)
    hidden(0)
    weight_z(0)
    gc_ref[pl.ds(pl.multiple_of(y * 32, 32), 32), :] = cback[y]
    arrived(col_keep, ("gc",))
    for d in (1, 2, 3):
        gc_ref[pl.ds(pl.multiple_of(on_y(4 - d) * 32, 32), 32), :] = col_keep[d - 1]
    weight_z(1)
    arrived(hgot, ("hid",))
    gh_ref[...] = hpart[0] + hgot[0] + hgot[1] + hgot[2]
    total = wpart[7, x, c]
    arrived(wgot_z, ("wz",))
    for d in order[:7]:
        total = total + wgot_z[d - 1]
    gw_ref[...] = total
    for group, tiles in enumerate(groups):
        whole = blank.at[pl.ds(0, tiles)]
        pltpu.make_async_remote_copy(
            src_ref=whole, dst_ref=whole, send_sem=ss.at[group], recv_sem=rs.at[0],
            device_id=partner, device_id_type=MESH,
        ).wait_send()


def body(text_hidden, proj_weight, clip_embed, positive, logit_scale):
    whole = pl.BlockSpec(memory_space=pl.ANY)
    vmem = pl.BlockSpec(memory_space=pltpu.VMEM)
    scratch = [
        ((4, 4, 2, 128, 256), F32), ((4, 4, 256, 256), BF16), ((4, 4, 256, 256), BF16),
        ((8, 4, 32, 256), F32), ((4, 256, 256), BF16), ((4, 256, 256), BF16),
        ((2, 4, 8, 128), jnp.int32), ((4, 8, 256), F32),
        ((4, 256, 256), F32), ((4, 256, 256), F32), ((4, 256, 256), F32), ((4, 8, 256), F32), ((4, 8, 256), F32),
        ((3, 16, 128), F32), ((7, 16, 128), F32), ((3, 16, 128), F32),
        ((8, 128), F32), ((7, 8, 128), F32), ((3, 32, 256), F32), ((4, 8, 256), F32),
        ((4, 256, 256), BF16), ((4, 256, 256), BF16),
        ((4, 4, 2, 128, 256), F32), ((4, 4, 128, 256), F32),
        ((2, 4, 32, 256), F32), ((2, 4, 32, 256), F32), ((2, 4, 64, 256), F32), ((2, 4, 64, 256), F32),
        ((3, 64, 256), F32), ((3, 64, 256), F32),
        ((8, 128), F32), ((8, 128), F32), ((8, 128), F32), ((3, 8, 128), F32), ((8, 128), F32), ((3, 8, 128), F32),
        ((8, 4, 32, 256), F32), ((2, 4, 4, 32, 256), F32),
        ((4, 128, 256), F32), ((3, 128, 256), F32),
        ((8, 4, 2, 16, 256), F32), ((8, 4, 16, 256), F32), ((3, 8, 16, 256), F32), ((7, 16, 256), F32),
        ((4, 32, 256), F32), ((128, 1024), F32), ((1024, 256), F32), ((GROUP_TILES, 8, 128), F32),
    ]
    return pl.pallas_call(
        kernel,
        out_shape=(
            pltpu.VMEM((128, 256), F32),
            pltpu.VMEM((16, 256), F32),
            pltpu.VMEM((128, 256), F32),
        ),
        in_specs=[whole, whole, vmem, vmem, pl.BlockSpec(memory_space=pltpu.SMEM)],
        out_specs=(vmem, vmem, vmem),
        scratch_shapes=[pltpu.VMEM(shape, dtype) for shape, dtype in scratch]
        + [pltpu.SemaphoreType.DMA((n,)) for n in (GROUPS, COUNT, 2)],
        compiler_params=pltpu.CompilerParams(
            collective_id=0, has_side_effects=True, vmem_limit_bytes=56 << 20
        ),
        name="contrastive",
    )(text_hidden, proj_weight, clip_embed, positive.reshape(1, 128), logit_scale)


def solution(mesh):
    rows = ("txt", "clip")
    in_specs = (P(rows, None), P(None, "proj"), P(rows, "proj"), P(rows), P())
    out_specs = (P(rows, "proj"), P(rows, "proj"), P(rows, "proj"))
    return jax.shard_map(body, mesh=mesh, in_specs=in_specs, out_specs=out_specs, check_vma=False)
```

```python
import math

import jax
import jax.numpy as jnp
from jax import lax
from jax.experimental import pallas as pl
from jax.experimental.pallas import tpu as pltpu
from jax.sharding import PartitionSpec as P

MESH = pl.DeviceIdType.MESH
EPSILON = 1e-06
PRECISE = lax.Precision.HIGHEST
F32 = jnp.float32
BF16 = jnp.bfloat16

COUNT = 134
GROUPS = 3
GROUP_TILES = 1024
TURN = (1, 3)
CAME = (3, 1)
CHUNKS = (2, 1, 3, 0)


def split(value):
    high = value.astype(BF16)
    return high, (value - high.astype(F32)).astype(BF16)


def product(a, b, dims):
    return lax.dot_general(a, b, (dims, ((), ())), preferred_element_type=F32)


def product3(a, b, dims):
    (ah, al), (bh, bl) = a, b
    return product(ah, bh, dims) + product(ah, bl, dims) + product(al, bh, dims)


def exact(a, b, dims):
    return lax.dot_general(a, b, (dims, ((), ())), precision=PRECISE, preferred_element_type=F32)


def turned(column):
    return jnp.broadcast_to(column, (128, 128)).T[0:1, :]


def upright(line):
    return jnp.broadcast_to(line, (128, 128)).T[:, 0:1]


def joined(stats):
    top = stats[0][0]
    for part in stats[1:]:
        top = jnp.maximum(top, part[0])
    total = stats[0][1] * jnp.exp(stats[0][0] - top)
    for part in stats[1:]:
        total = total + part[1] * jnp.exp(part[0] - top)
    return top, total


def kernel(
    hid_hbm, w_hbm, clip_ref, pos_ref, scale_ref,
    gh_ref, gw_ref, gc_ref,
    text, text_h, text_l, clip, clip_h, clip_l, pos, inv_t, scores, exp_r, exp_c, max_t, sum_t,
    row_stat, row_got_y, row_got_x, col_stat, col_got, col_keep, fac_t, g_h, g_l,
    part, part_c, got_aa, got_bb, got_a, got_b, got_ya, got_xb,
    along_own, along_c, along_pair, along_y, along_sum, along_x, cpart, cgot, hpart, hgot, wpart, wgot_c, wgot_x, wgot_z,
    cback, hid_ref, w_ref, hid_h, hid_l, w_h, w_l, blank, ss, rs, ls,
):
    z = lax.axis_index("txt")
    k = lax.axis_index("clip")
    y = lax.axis_index("proj")
    x = k // 2
    c = lax.rem(k, 2)
    o = 1 - c

    def on_z(d):
        return lax.rem(z + d, 8)

    def on_x(d):
        return lax.rem(x + d, 4)

    def on_y(d):
        return lax.rem(y + d, 4)

    partner = (z, 2 * x + o, y)

    def z_peer(d):
        return (on_z(d), k, y)

    def x_peer(d):
        return (z, 2 * on_x(d) + c, y)

    def y_peer(d):
        return (z, k, on_y(d))

    def y_other(d):
        return (z, 2 * x + o, on_y(d))

    groups = [0]
    places = {}

    def slot(key):
        return places.setdefault(key, len(places))

    def copy_of(src, dst, key, device):
        return pltpu.make_async_remote_copy(
            src_ref=src, dst_ref=dst, send_sem=ss.at[len(groups) - 1], recv_sem=rs.at[slot(key)],
            device_id=device, device_id_type=MESH,
        )

    def send(src, dst, key, device):
        tiles = math.prod(src.shape) // 1024
        if groups[-1] + tiles > GROUP_TILES:
            groups.append(0)
        groups[-1] += tiles
        copy_of(src, dst, key, device).start()

    def arrived(place, key):
        copy_of(place, place, key, partner).wait_recv()

    peers = [partner] + [y_peer(d) for d in (1, 2, 3)] + [x_peer(d) for d in (1, 2, 3)]
    peers += [z_peer(d) for d in range(1, 8)] + [y_other(d) for d in (1, 2, 3)]
    barrier = pltpu.get_barrier_semaphore()
    for device in peers:
        pl.semaphore_signal(barrier, inc=1, device_id=device, device_id_type=MESH)
    loads = [
        pltpu.make_async_copy(hid_hbm, hid_ref, ls.at[0]),
        pltpu.make_async_copy(w_hbm, w_ref, ls.at[1]),
    ]
    for load in loads:
        load.start()
    scale = scale_ref[0]
    pos[c, x] = jnp.broadcast_to(pos_ref[...], (8, 128))
    clip[z, y] = clip_ref[pl.ds(pl.multiple_of(y * 32, 32), 32), :]
    for load in loads:
        load.wait()
    text[y, x, c] = exact(hid_ref[...], w_ref[...], ((1,), (0,)))
    hid_h[...], hid_l[...] = split(hid_ref[...])
    w_h[...], w_l[...] = split(w_ref[...])
    pl.semaphore_wait(barrier, len(peers))

    for d in (1, 2, 3):
        rows = pl.ds(pl.multiple_of(on_y(d) * 32, 32), 32)
        send(clip_ref.at[rows], clip.at[z, y], ("clip_y", d), y_peer(d))
    for d in (1, 2, 3):
        send(pos.at[c, x], pos.at[c, x], ("pos_x", d - 1), x_peer(d))

    def rows_of(kind, part=None):
        return pl.ds(64 * kind, 64) if part is None else pl.ds(64 * kind + 32 * part, 32)

    def block_of(kind, near, far, part=None):
        dy, dx = (far, near) if kind == 0 else (near, far)
        return text.at[on_y(dy), on_x(dx), c, rows_of(kind, part)]

    def near_peer(kind, d):
        return x_peer(d) if kind == 0 else y_peer(d)

    def far_peer(kind, d):
        return y_peer(d) if kind == 0 else x_peer(d)

    def spread(block, key, device):
        send(block, block, key, device)

    def begin(kind):
        for way in (0, 1):
            spread(block_of(kind, 0, 0), ("n", kind, way), near_peer(kind, TURN[way]))

    def cross(kind, e):
        for way in (0, 1):
            spread(block_of(kind, e, 0), ("f", kind, e, way), far_peer(kind, TURN[way]))

    def relay_near(kind):
        for way in (0, 1):
            arrived(block_of(kind, CAME[way], 0), ("n", kind, way))
            spread(block_of(kind, CAME[way], 0, way), ("nn", kind), near_peer(kind, TURN[way]))

    def relay_far(kind, e):
        for way in (0, 1):
            arrived(block_of(kind, e, CAME[way]), ("f", kind, e, way))
            spread(block_of(kind, e, CAME[way], way), ("ff", kind, e), far_peer(kind, TURN[way]))

    def last_piece(kind, e, core):
        return text.at[on_y(2), on_x(e), core, rows_of(0)] if kind == 0 else text.at[on_y(e), on_x(2), core, rows_of(1)]

    def group_of(kind, far, core):
        rows = rows_of(kind)
        return text.at[on_y(far), :, core, rows] if kind == 0 else text.at[:, on_x(far), core, rows]

    def to_partner(kind, far):
        spread(group_of(kind, far, c), ("p", kind, far), partner)

    def clip_piece(far, d):
        return clip.at[on_z(far), on_y(d)]

    def ring_clip(step, d):
        for way in (0, 1):
            if step > 1:
                ring_clip_wait(step - 1, d, way)
            if step < 4 or d in ((0, 3), (1, 2))[way]:
                block = clip_piece(9 - step if way == 0 else step - 1, d)
                spread(block, ("gz", step, d, way), z_peer(1 if way == 0 else 7))

    def ring_clip_wait(step, d, way):
        arrived(clip_piece(8 - step if way == 0 else step, d), ("gz", step, d, way))

    ring_clip(1, 0)
    for kind in (0, 1):
        begin(kind)
    for kind in (0, 1):
        cross(kind, 0)
    for d in (1, 3, 2):
        arrived(clip_piece(0, d), ("clip_y", 4 - d))
        ring_clip(1, d)
    for d in (1, 2, 3):
        arrived(pos.at[c, on_x(4 - d)], ("pos_x", d - 1))
    send(pos.at[c], pos.at[c], ("pos_c", 0), partner)
    ring_clip(2, 0)
    for kind in (0, 1):
        relay_near(kind)
        for e in CAME:
            cross(kind, e)
    for d in (1, 3, 2):
        ring_clip(2, d)
    for kind in (0, 1):
        relay_far(kind, 0)
    ring_clip(3, 0)
    for kind in (0, 1):
        arrived(block_of(kind, 2, 0), ("nn", kind))
        cross(kind, 2)
    for d in (1, 3, 2):
        ring_clip(3, d)
    for kind in (0, 1):
        to_partner(kind, 0)
        for e in CAME:
            relay_far(kind, e)
    ring_clip(4, 0)
    for d in (1, 3, 2):
        ring_clip(4, d)
    for kind in (0, 1):
        relay_far(kind, 2)
        for d in CAME:
            to_partner(kind, d)
    for e in (0, 1, 3, 2):
        for kind in (0, 1):
            arrived(last_piece(kind, e, c), ("ff", kind, e))
            spread(last_piece(kind, e, c), ("q", kind), partner)
    for d in (0, 1, 3, 2):
        ring_clip_wait(4, d, 0 if d in (0, 3) else 1)

    def clip_block(f, squares):
        block = clip[:, f].reshape(256, 256)
        clip_h[f], clip_l[f] = split(block)
        return squares + jnp.sum(block * block, axis=1, keepdims=True)

    inv_c = lax.rsqrt(lax.fori_loop(0, 4, clip_block, jnp.zeros((256, 1), F32)) + EPSILON)
    col_scale = scale * inv_c

    for d in (0, 1, 3, 2):
        for kind in (0, 1):
            arrived(group_of(kind, d, o), ("p", kind, d) if d != 2 else ("q", kind))
    arrived(pos.at[o], ("pos_c", 0))

    def score(q, carry):
        squares = jnp.zeros((256, 1), F32)
        total = jnp.zeros((256, 256), F32)
        for f in range(4):
            block = text[f, q].reshape(256, 256)
            high, low = split(block)
            text_h[f, q], text_l[f, q] = high, low
            squares = squares + jnp.sum(block * block, axis=1, keepdims=True)
            total = total + product3((clip_h[f], clip_l[f]), (high, low), ((1,), (1,)))
        inverse = lax.rsqrt(squares + EPSILON)
        lanes = jnp.concatenate([turned(inverse[0:128]), turned(inverse[128:256])], axis=1)
        inv_t[q] = jnp.broadcast_to(lanes, (8, 256))
        tile = total * col_scale * lanes
        scores[q] = tile
        top = jnp.max(tile, axis=0, keepdims=True)
        raised = jnp.exp(tile - top)
        exp_r[q] = raised
        max_t[q] = jnp.broadcast_to(top, (8, 256))
        sum_t[q] = jnp.broadcast_to(jnp.sum(raised, axis=0, keepdims=True), (8, 256))
        return carry

    lax.fori_loop(0, 4, score, 0)

    for q in range(4):
        for h in (0, 1):
            row = 2 * q + h
            row_stat[0, row : row + 1, :] = max_t[q, 0:1, h * 128 : h * 128 + 128]
            row_stat[0, 8 + row : 9 + row, :] = sum_t[q, 0:1, h * 128 : h * 128 + 128]
    send(row_stat.at[0], row_got_y.at[0], ("stat",), partner)
    for d in (2, 1, 3):
        send(row_stat.at[0], row_got_y.at[d], ("stat",), y_peer(d))
        send(row_stat.at[0], row_got_y.at[3 + d], ("stat",), y_other(d))
    top_c = jnp.max(scores[0], axis=1, keepdims=True)
    for q in range(1, 4):
        top_c = jnp.maximum(top_c, jnp.max(scores[q], axis=1, keepdims=True))
    total_c = jnp.zeros((256, 1), F32)
    for q in range(4):
        raised = jnp.exp(scores[q] - top_c)
        exp_c[q] = raised
        total_c = total_c + jnp.sum(raised, axis=1, keepdims=True)
    for h in (0, 1):
        col_stat[h : h + 1, :] = turned(top_c[h * 128 : h * 128 + 128])
        col_stat[2 + h : 3 + h, :] = turned(total_c[h * 128 : h * 128 + 128])
    col_stat[4:8, :] = jnp.zeros((4, 128), F32)
    for d in range(1, 8):
        send(col_stat, col_got.at[d - 1], ("stat_z",), z_peer(d))

    def row_part(value):
        return value[0:8], value[8:16]

    arrived(row_got_y, ("stat",))
    stats = joined([row_part(row_stat[0])] + [row_part(row_got_y[d]) for d in range(7)])
    row_stat[2, 0:8], row_stat[2, 8:16] = stats
    for d in (1, 3, 2):
        send(row_stat.at[2], row_got_x.at[d - 1], ("stat_x",), x_peer(d))
    arrived(col_got, ("stat_z",))

    def col_part(value):
        return value[0:2], value[2:4]

    top_g, total_g = joined([col_part(col_stat[...])] + [col_part(col_got[d]) for d in range(7)])
    fac = 0.5 * jnp.exp(col_stat[0:2] - top_g) / total_g
    fac_c = jnp.concatenate([upright(fac[0:1]), upright(fac[1:2])], axis=0)
    arrived(row_got_x, ("stat_x",))
    top_g, total_g = joined([stats] + [row_part(row_got_x[d]) for d in range(3)])
    fac = 0.5 * jnp.exp(row_stat[0, 0:8] - top_g) / total_g
    for q in range(4):
        for h in (0, 1):
            row = 2 * q + h
            fac_t[q, :, h * 128 : h * 128 + 128] = jnp.broadcast_to(fac[row : row + 1], (8, 128))

    number = lax.broadcasted_iota(jnp.int32, (256, 256), 0)
    clip_id = lax.shift_right_logical(number, 5) * 1024 + (number & 31) + (k * 128 + y * 32)

    def gradient(i):
        q = on_x(CHUNKS[i])
        target = jnp.concatenate([pos[0, q, 0:1, :], pos[1, q, 0:1, :]], axis=1)
        grad = exp_r[q] * fac_t[q, 0:1, :] + exp_c[q] * fac_c
        grad = grad - (clip_id == target).astype(F32)
        line = jnp.sum(grad * scores[q], axis=0, keepdims=True)
        for h in (0, 1):
            along_own[2 * i + h : 2 * i + h + 1, :] = line[:, h * 128 : h * 128 + 128]
        g_h[q], g_l[q] = split(grad * (scale * inv_t[q, 0:1, :]))
        weighted = split(grad * col_scale)
        for f in range(4):
            block = product3(weighted, (clip_h[f], clip_l[f]), ((0,), (0,)))
            part[f, q] = block.reshape(2, 128, 256)
        send(part.at[:, q, o], part_c.at[:, q], ("rc", i), partner)

    for i in range(4):
        gradient(i)
    send(along_own, along_c, ("along_c", 0), partner)

    def clip_gradient(f, carry):
        total = jnp.zeros((256, 256), F32)
        for q in range(4):
            total = total + product3((g_h[q], g_l[q]), (text_h[f, q], text_l[f, q]), ((1,), (0,)))
        cpart[:, f] = total.reshape(8, 32, 256)
        return carry

    lax.fori_loop(0, 4, clip_gradient, 0)

    def ring_sum(step):
        for f in range(4):
            for way in (0, 1):
                goal = on_z(5 - step) if way == 0 else on_z(3 + step)
                if step > 2 or (step == 2 and f // 2 == way):
                    place = cgot.at[way, step - 2, f]
                    arrived(place, ("cz", step - 1, f, way))
                    cpart[goal, f] = cpart[goal, f] + place[...]
                if step > 1 or f // 2 == way:
                    send(
                        cpart.at[goal, f], cgot.at[way, step - 1, f],
                        ("cz", step, f if step < 4 else 0, way), z_peer(1 if way == 0 else 7),
                    )

    def half_of(part):
        return pl.ds(32 * part, 32)

    def pass_a(d, way, half):
        send(
            part.at[:, on_x(d), c, rows_of(0, half)], got_a.at[way, :, half_of(half)],
            ("ra", way), x_peer(TURN[way]),
        )

    def pass_b(i, d, way, half):
        send(
            part.at[on_y(d), on_x(CHUNKS[i]), c, rows_of(1, half)], got_b.at[way, i, half_of(half)],
            ("rb", i, way), y_peer(TURN[way]),
        )

    def join_cores(i):
        q = on_x(CHUNKS[i])
        arrived(part_c.at[:, q], ("rc", i))
        for f in range(4):
            part[f, q, c] = part[f, q, c] + part_c[f, q]
        for way in (0, 1):
            if i == 0:
                send(
                    part.at[:, q, c, rows_of(0, way)], got_aa.at[way], ("raa", way), x_peer(TURN[way])
                )
            if CHUNKS[i] == TURN[way]:
                pass_a(TURN[way], way, 1 - way)
            send(
                part.at[on_y(2), q, c, rows_of(1, way)], got_bb.at[way, i], ("rbb", i, way),
                y_peer(TURN[way]),
            )
        for way in (0, 1):
            pass_b(i, TURN[way], way, 1 - way)

    def relay_a():
        for way in (0, 1):
            arrived(got_aa.at[way], ("raa", way))
            at = slice(32 * way, 32 * way + 32)
            for f in range(4):
                part[f, on_x(TURN[way]), c, at] = part[f, on_x(TURN[way]), c, at] + got_aa[way, f]
            pass_a(TURN[way], way, way)

    def relay_b(i):
        q = on_x(CHUNKS[i])
        for way in (0, 1):
            arrived(got_bb.at[way, i], ("rbb", i, way))
            at = slice(64 + 32 * way, 96 + 32 * way)
            part[on_y(TURN[way]), q, c, at] = part[on_y(TURN[way]), q, c, at] + got_bb[way, i]
            pass_b(i, TURN[way], way, way)

    def finish_a():
        for way in (0, 1):
            arrived(got_a.at[way], ("ra", way))
        for d in (2, 1, 3, 0):
            e = on_y(d)
            part[e, x, c, 0:64] = part[e, x, c, 0:64] + got_a[0, e] + got_a[1, e]
            if d > 0:
                send(part.at[e, x, c, rows_of(0)], got_ya.at[d - 1], ("ya",), y_peer(d))

    def finish_b(i):
        q = on_x(CHUNKS[i])
        for way in (0, 1):
            arrived(got_b.at[way, i], ("rb", i, way))
        part[y, q, c, 64:128] = part[y, q, c, 64:128] + got_b[0, i] + got_b[1, i]
        d = CHUNKS[i]
        if d > 0:
            send(part.at[y, q, c, rows_of(1)], got_xb.at[d - 1], ("xb",), x_peer(d))

    join_cores(0)
    ring_sum(1)
    join_cores(1)
    join_cores(2)
    join_cores(3)
    arrived(along_c, ("along_c", 0))
    along_pair[...] = along_own[...] + along_c[...]
    for d in (2, 1, 3):
        send(along_pair, along_y.at[d - 1], ("along_y",), y_peer(d))
    relay_a()
    relay_b(0)
    ring_sum(2)
    relay_b(1)
    relay_b(2)
    arrived(along_y, ("along_y",))
    along_sum[...] = along_pair[...] + along_y[0] + along_y[1] + along_y[2]
    for d in (2, 1, 3):
        send(along_sum, along_x.at[d - 1], ("along_x",), x_peer(d))
    relay_b(3)
    ring_sum(3)
    finish_b(0)
    finish_a()
    for i in (1, 2, 3):
        finish_b(i)
    ring_sum(4)

    def clip_rows():
        for way in (0, 1):
            arrived(cgot.at[way, 3], ("cz", 4, 0, way))
        squares = jnp.zeros((32, 1), F32)
        along = jnp.zeros((32, 1), F32)
        for f in range(4):
            total = cpart[z, f] + cgot[0, 3, f] + cgot[1, 3, f]
            raw = clip[z, f]
            cback[f] = total
            squares = squares + jnp.sum(raw * raw, axis=1, keepdims=True)
            along = along + jnp.sum(raw * total, axis=1, keepdims=True)
        inverse = lax.rsqrt(squares + EPSILON)
        for f in range(4):
            cback[f] = (cback[f] - (clip[z, f] * inverse) * (along * inverse)) * inverse
        for d in (1, 3, 2):
            send(cback.at[on_y(d)], col_keep.at[d - 1], ("gc",), y_peer(d))

    squares = jnp.zeros((128, 1), F32)
    for f in range(4):
        raw = text[f, x, c]
        squares = squares + jnp.sum(raw * raw, axis=1, keepdims=True)
    inverse = lax.rsqrt(squares + EPSILON)
    arrived(got_ya, ("ya",))
    arrived(got_xb, ("xb",))
    arrived(along_x, ("along_x",))
    lines = along_sum[6:8]
    for d in (1, 2, 3):
        at = 2 * CHUNKS.index(d)
        lines = lines + along_x[d - 1, at : at + 2]
    along = upright(jnp.where(c == 0, lines[0:1], lines[1:2]))
    upper = part[y, x, c, 0:64] + got_ya[0] + got_ya[1] + got_ya[2]
    lower = part[y, x, c, 64:128] + got_xb[0] + got_xb[1] + got_xb[2]
    cot = jnp.concatenate([upper, lower], axis=0)
    back = (cot - (text[y, x, c] * inverse) * along) * inverse

    order = (4, 3, 5, 2, 6, 1, 7, 0)
    back_parts = split(back)

    def weight(t):
        for j in range(4 * t, 4 * t + 4):
            rows = pl.ds(pl.multiple_of(on_z(order[j]) * 128, 128), 128)
            block = product3((hid_h[:, rows], hid_l[:, rows]), back_parts, ((0,), (0,)))
            wpart[j] = block.reshape(4, 2, 16, 256)
        send(wpart.at[4 * t : 4 * t + 4, :, o], wgot_c.at[4 * t : 4 * t + 4], ("wc", t), partner)

    def hidden(d):
        rows = pl.ds(pl.multiple_of(on_y(d) * 256, 256), 256)
        hpart[d] = product3(back_parts, (w_h[rows, :], w_l[rows, :]), ((1,), (1,)))
        if d > 0:
            send(hpart.at[d], hgot.at[d - 1], ("hid",), y_peer(d))

    def weight_x(t):
        arrived(wgot_c.at[4 * t : 4 * t + 4], ("wc", t))
        for j in range(4 * t, 4 * t + 4):
            for f in range(4):
                wpart[j, f, c] = wpart[j, f, c] + wgot_c[j, f]
        for d in (2, 1, 3):
            send(
                wpart.at[4 * t : 4 * t + 4, on_x(d), c], wgot_x.at[d - 1, 4 * t : 4 * t + 4],
                ("wx", t), x_peer(d),
            )

    def weight_z(t):
        arrived(wgot_x.at[:, 4 * t : 4 * t + 4], ("wx", t))
        for j in range(4 * t, 4 * t + 4):
            wpart[j, x, c] = wpart[j, x, c] + wgot_x[0, j] + wgot_x[1, j] + wgot_x[2, j]
            d = order[j]
            if d > 0:
                send(wpart.at[j, x, c], wgot_z.at[d - 1], ("wz",), z_peer(d))

    weight(0)
    hidden(2)
    weight(1)
    weight_x(0)
    hidden(1)
    hidden(3)
    weight_x(1)
    clip_rows()
    hidden(0)
    weight_z(0)
    gc_ref[pl.ds(pl.multiple_of(y * 32, 32), 32), :] = cback[y]
    arrived(col_keep, ("gc",))
    for d in (1, 2, 3):
        gc_ref[pl.ds(pl.multiple_of(on_y(4 - d) * 32, 32), 32), :] = col_keep[d - 1]
    weight_z(1)
    arrived(hgot, ("hid",))
    gh_ref[...] = hpart[0] + hgot[0] + hgot[1] + hgot[2]
    total = wpart[7, x, c]
    arrived(wgot_z, ("wz",))
    for d in order[:7]:
        total = total + wgot_z[d - 1]
    gw_ref[...] = total
    for group, tiles in enumerate(groups):
        whole = blank.at[pl.ds(0, tiles)]
        pltpu.make_async_remote_copy(
            src_ref=whole, dst_ref=whole, send_sem=ss.at[group], recv_sem=rs.at[0],
            device_id=partner, device_id_type=MESH,
        ).wait_send()


def body(text_hidden, proj_weight, clip_embed, positive, logit_scale):
    whole = pl.BlockSpec(memory_space=pl.ANY)
    vmem = pl.BlockSpec(memory_space=pltpu.VMEM)
    scratch = [
        ((4, 4, 2, 128, 256), F32), ((4, 4, 256, 256), BF16), ((4, 4, 256, 256), BF16),
        ((8, 4, 32, 256), F32), ((4, 256, 256), BF16), ((4, 256, 256), BF16),
        ((2, 4, 8, 128), jnp.int32), ((4, 8, 256), F32),
        ((4, 256, 256), F32), ((4, 256, 256), F32), ((4, 256, 256), F32), ((4, 8, 256), F32), ((4, 8, 256), F32),
        ((3, 16, 128), F32), ((7, 16, 128), F32), ((3, 16, 128), F32),
        ((8, 128), F32), ((7, 8, 128), F32), ((3, 32, 256), F32), ((4, 8, 256), F32),
        ((4, 256, 256), BF16), ((4, 256, 256), BF16),
        ((4, 4, 2, 128, 256), F32), ((4, 4, 128, 256), F32),
        ((2, 4, 32, 256), F32), ((2, 4, 32, 256), F32), ((2, 4, 64, 256), F32), ((2, 4, 64, 256), F32),
        ((3, 64, 256), F32), ((3, 64, 256), F32),
        ((8, 128), F32), ((8, 128), F32), ((8, 128), F32), ((3, 8, 128), F32), ((8, 128), F32), ((3, 8, 128), F32),
        ((8, 4, 32, 256), F32), ((2, 4, 4, 32, 256), F32),
        ((4, 128, 256), F32), ((3, 128, 256), F32),
        ((8, 4, 2, 16, 256), F32), ((8, 4, 16, 256), F32), ((3, 8, 16, 256), F32), ((7, 16, 256), F32),
        ((4, 32, 256), F32), ((128, 1024), F32), ((1024, 256), F32),
        ((128, 1024), BF16), ((128, 1024), BF16), ((1024, 256), BF16), ((1024, 256), BF16), ((GROUP_TILES, 8, 128), F32),
    ]
    return pl.pallas_call(
        kernel,
        out_shape=(
            pltpu.VMEM((128, 256), F32),
            pltpu.VMEM((16, 256), F32),
            pltpu.VMEM((128, 256), F32),
        ),
        in_specs=[whole, whole, vmem, vmem, pl.BlockSpec(memory_space=pltpu.SMEM)],
        out_specs=(vmem, vmem, vmem),
        scratch_shapes=[pltpu.VMEM(shape, dtype) for shape, dtype in scratch]
        + [pltpu.SemaphoreType.DMA((n,)) for n in (GROUPS, COUNT, 2)],
        compiler_params=pltpu.CompilerParams(
            collective_id=0, has_side_effects=True, vmem_limit_bytes=56 << 20
        ),
        name="contrastive",
    )(text_hidden, proj_weight, clip_embed, positive.reshape(1, 128), logit_scale)


def solution(mesh):
    rows = ("txt", "clip")
    in_specs = (P(rows, None), P(None, "proj"), P(rows, "proj"), P(rows), P())
    out_specs = (P(rows, "proj"), P(rows, "proj"), P(rows, "proj"))
    return jax.shard_map(body, mesh=mesh, in_specs=in_specs, out_specs=out_specs, check_vma=False)
```

```python
import math

import jax
import jax.numpy as jnp
from jax import lax
from jax.experimental import pallas as pl
from jax.experimental.pallas import tpu as pltpu
from jax.sharding import PartitionSpec as P

MESH = pl.DeviceIdType.MESH
EPSILON = 1e-06
PRECISE = lax.Precision.HIGHEST
F32 = jnp.float32
BF16 = jnp.bfloat16

COUNT = 134
GROUPS = 3
GROUP_TILES = 1024
TURN = (1, 3)
CAME = (3, 1)
CHUNKS = (2, 1, 3, 0)


def split(value):
    high = value.astype(BF16)
    return high, (value - high.astype(F32)).astype(BF16)


def product(a, b, dims):
    return lax.dot_general(a, b, (dims, ((), ())), preferred_element_type=F32)


def product3(a, b, dims):
    (ah, al), (bh, bl) = a, b
    return product(ah, bh, dims) + product(ah, bl, dims) + product(al, bh, dims)


def exact(a, b, dims):
    return lax.dot_general(a, b, (dims, ((), ())), precision=PRECISE, preferred_element_type=F32)


def turned(column):
    return jnp.broadcast_to(column, (128, 128)).T[0:1, :]


def upright(line):
    return jnp.broadcast_to(line, (128, 128)).T[:, 0:1]


def joined(stats):
    top = stats[0][0]
    for part in stats[1:]:
        top = jnp.maximum(top, part[0])
    total = stats[0][1] * jnp.exp(stats[0][0] - top)
    for part in stats[1:]:
        total = total + part[1] * jnp.exp(part[0] - top)
    return top, total


def kernel(
    hid_hbm, w_hbm, clip_ref, pos_ref, scale_ref,
    gh_ref, gw_ref, gc_ref,
    text, text_h, text_l, clip, clip_h, clip_l, pos, inv_t, scores, exp_r, exp_c, max_t, sum_t,
    row_stat, row_got_y, row_got_x, col_stat, col_got, col_keep, fac_t, g_h, g_l,
    part, part_c, got_aa, got_bb, got_a, got_b, got_ya, got_xb,
    along_own, along_c, along_pair, along_y, along_sum, along_x, cpart, cgot, hpart, hgot, wpart, wgot_c, wgot_x, wgot_z,
    cback, hid_ref, w_ref, hid_h, hid_l, w_h, w_l, blank, ss, rs, ls,
):
    z = lax.axis_index("txt")
    k = lax.axis_index("clip")
    y = lax.axis_index("proj")
    x = k // 2
    c = lax.rem(k, 2)
    o = 1 - c

    def on_z(d):
        return lax.rem(z + d, 8)

    def on_x(d):
        return lax.rem(x + d, 4)

    def on_y(d):
        return lax.rem(y + d, 4)

    partner = (z, 2 * x + o, y)

    def z_peer(d):
        return (on_z(d), k, y)

    def x_peer(d):
        return (z, 2 * on_x(d) + c, y)

    def y_peer(d):
        return (z, k, on_y(d))

    def y_other(d):
        return (z, 2 * x + o, on_y(d))

    groups = [0]
    places = {}

    def slot(key):
        return places.setdefault(key, len(places))

    def copy_of(src, dst, key, device):
        return pltpu.make_async_remote_copy(
            src_ref=src, dst_ref=dst, send_sem=ss.at[len(groups) - 1], recv_sem=rs.at[slot(key)],
            device_id=device, device_id_type=MESH,
        )

    def send(src, dst, key, device):
        tiles = math.prod(src.shape) // 1024
        if groups[-1] + tiles > GROUP_TILES:
            groups.append(0)
        groups[-1] += tiles
        copy_of(src, dst, key, device).start()

    def arrived(place, key):
        copy_of(place, place, key, partner).wait_recv()

    peers = [partner] + [y_peer(d) for d in (1, 2, 3)] + [x_peer(d) for d in (1, 2, 3)]
    peers += [z_peer(d) for d in range(1, 8)] + [y_other(d) for d in (1, 2, 3)]
    barrier = pltpu.get_barrier_semaphore()
    for device in peers:
        pl.semaphore_signal(barrier, inc=1, device_id=device, device_id_type=MESH)
    loads = [
        pltpu.make_async_copy(hid_hbm, hid_ref, ls.at[0]),
        pltpu.make_async_copy(w_hbm, w_ref, ls.at[1]),
    ]
    for load in loads:
        load.start()
    scale = scale_ref[0]
    pos[c, x] = jnp.broadcast_to(pos_ref[...], (8, 128))
    clip[z, y] = clip_ref[pl.ds(pl.multiple_of(y * 32, 32), 32), :]
    for load in loads:
        load.wait()
    text[y, x, c] = exact(hid_ref[...], w_ref[...], ((1,), (0,)))
    hid_h[...], hid_l[...] = split(hid_ref[...])
    w_h[...], w_l[...] = split(w_ref[...])
    pl.semaphore_wait(barrier, len(peers))

    for d in (1, 2, 3):
        rows = pl.ds(pl.multiple_of(on_y(d) * 32, 32), 32)
        send(clip_ref.at[rows], clip.at[z, y], ("clip_y", d), y_peer(d))
    for d in (1, 2, 3):
        send(pos.at[c, x], pos.at[c, x], ("pos_x", d - 1), x_peer(d))

    def rows_of(kind, part=None):
        return pl.ds(64 * kind, 64) if part is None else pl.ds(64 * kind + 32 * part, 32)

    def block_of(kind, near, far, part=None):
        dy, dx = (far, near) if kind == 0 else (near, far)
        return text.at[on_y(dy), on_x(dx), c, rows_of(kind, part)]

    def near_peer(kind, d):
        return x_peer(d) if kind == 0 else y_peer(d)

    def far_peer(kind, d):
        return y_peer(d) if kind == 0 else x_peer(d)

    def spread(block, key, device):
        send(block, block, key, device)

    def begin(kind):
        for way in (0, 1):
            spread(block_of(kind, 0, 0), ("n", kind, way), near_peer(kind, TURN[way]))
        spread(block_of(kind, 0, 0), ("nn", kind), near_peer(kind, 2))

    def cross(kind, e):
        for way in (0, 1):
            spread(block_of(kind, e, 0), ("f", kind, e, way), far_peer(kind, TURN[way]))

    def relay_near(kind):
        for way in (0, 1):
            arrived(block_of(kind, CAME[way], 0), ("n", kind, way))

    def relay_far(kind, e):
        for way in (0, 1):
            arrived(block_of(kind, e, CAME[way]), ("f", kind, e, way))
            spread(block_of(kind, e, CAME[way], way), ("ff", kind, e), far_peer(kind, TURN[way]))

    def last_piece(kind, e, core):
        return text.at[on_y(2), on_x(e), core, rows_of(0)] if kind == 0 else text.at[on_y(e), on_x(2), core, rows_of(1)]

    def group_of(kind, far, core):
        rows = rows_of(kind)
        return text.at[on_y(far), :, core, rows] if kind == 0 else text.at[:, on_x(far), core, rows]

    def to_partner(kind, far):
        spread(group_of(kind, far, c), ("p", kind, far), partner)

    def clip_piece(far, d):
        return clip.at[on_z(far), on_y(d)]

    def ring_clip(step, d):
        for way in (0, 1):
            if step > 1:
                ring_clip_wait(step - 1, d, way)
            if step < 4 or d in ((0, 3), (1, 2))[way]:
                block = clip_piece(9 - step if way == 0 else step - 1, d)
                spread(block, ("gz", step, d, way), z_peer(1 if way == 0 else 7))

    def ring_clip_wait(step, d, way):
        arrived(clip_piece(8 - step if way == 0 else step, d), ("gz", step, d, way))

    ring_clip(1, 0)
    for kind in (0, 1):
        begin(kind)
    for kind in (0, 1):
        cross(kind, 0)
    for d in (1, 3, 2):
        arrived(clip_piece(0, d), ("clip_y", 4 - d))
        ring_clip(1, d)
    for d in (1, 2, 3):
        arrived(pos.at[c, on_x(4 - d)], ("pos_x", d - 1))
    send(pos.at[c], pos.at[c], ("pos_c", 0), partner)
    ring_clip(2, 0)
    for kind in (0, 1):
        relay_near(kind)
        for e in CAME:
            cross(kind, e)
    for d in (1, 3, 2):
        ring_clip(2, d)
    for kind in (0, 1):
        relay_far(kind, 0)
    ring_clip(3, 0)
    for kind in (0, 1):
        arrived(block_of(kind, 2, 0), ("nn", kind))
        cross(kind, 2)
    for d in (1, 3, 2):
        ring_clip(3, d)
    for kind in (0, 1):
        to_partner(kind, 0)
        for e in CAME:
            relay_far(kind, e)
    ring_clip(4, 0)
    for d in (1, 3, 2):
        ring_clip(4, d)
    for kind in (0, 1):
        relay_far(kind, 2)
        for d in CAME:
            to_partner(kind, d)
    for e in (0, 1, 3, 2):
        for kind in (0, 1):
            arrived(last_piece(kind, e, c), ("ff", kind, e))
            spread(last_piece(kind, e, c), ("q", kind), partner)
    for d in (0, 1, 3, 2):
        ring_clip_wait(4, d, 0 if d in (0, 3) else 1)

    def clip_block(f, squares):
        block = clip[:, f].reshape(256, 256)
        clip_h[f], clip_l[f] = split(block)
        return squares + jnp.sum(block * block, axis=1, keepdims=True)

    inv_c = lax.rsqrt(lax.fori_loop(0, 4, clip_block, jnp.zeros((256, 1), F32)) + EPSILON)
    col_scale = scale * inv_c

    for d in (0, 1, 3, 2):
        for kind in (0, 1):
            arrived(group_of(kind, d, o), ("p", kind, d) if d != 2 else ("q", kind))
    arrived(pos.at[o], ("pos_c", 0))

    def score(q, carry):
        squares = jnp.zeros((256, 1), F32)
        total = jnp.zeros((256, 256), F32)
        for f in range(4):
            block = text[f, q].reshape(256, 256)
            high, low = split(block)
            text_h[f, q], text_l[f, q] = high, low
            squares = squares + jnp.sum(block * block, axis=1, keepdims=True)
            total = total + product3((clip_h[f], clip_l[f]), (high, low), ((1,), (1,)))
        inverse = lax.rsqrt(squares + EPSILON)
        lanes = jnp.concatenate([turned(inverse[0:128]), turned(inverse[128:256])], axis=1)
        inv_t[q] = jnp.broadcast_to(lanes, (8, 256))
        tile = total * col_scale * lanes
        scores[q] = tile
        top = jnp.max(tile, axis=0, keepdims=True)
        raised = jnp.exp(tile - top)
        exp_r[q] = raised
        max_t[q] = jnp.broadcast_to(top, (8, 256))
        sum_t[q] = jnp.broadcast_to(jnp.sum(raised, axis=0, keepdims=True), (8, 256))
        return carry

    lax.fori_loop(0, 4, score, 0)

    for q in range(4):
        for h in (0, 1):
            row = 2 * q + h
            row_stat[0, row : row + 1, :] = max_t[q, 0:1, h * 128 : h * 128 + 128]
            row_stat[0, 8 + row : 9 + row, :] = sum_t[q, 0:1, h * 128 : h * 128 + 128]
    send(row_stat.at[0], row_got_y.at[0], ("stat",), partner)
    for d in (2, 1, 3):
        send(row_stat.at[0], row_got_y.at[d], ("stat",), y_peer(d))
        send(row_stat.at[0], row_got_y.at[3 + d], ("stat",), y_other(d))
    top_c = jnp.max(scores[0], axis=1, keepdims=True)
    for q in range(1, 4):
        top_c = jnp.maximum(top_c, jnp.max(scores[q], axis=1, keepdims=True))
    total_c = jnp.zeros((256, 1), F32)
    for q in range(4):
        raised = jnp.exp(scores[q] - top_c)
        exp_c[q] = raised
        total_c = total_c + jnp.sum(raised, axis=1, keepdims=True)
    for h in (0, 1):
        col_stat[h : h + 1, :] = turned(top_c[h * 128 : h * 128 + 128])
        col_stat[2 + h : 3 + h, :] = turned(total_c[h * 128 : h * 128 + 128])
    col_stat[4:8, :] = jnp.zeros((4, 128), F32)
    for d in range(1, 8):
        send(col_stat, col_got.at[d - 1], ("stat_z",), z_peer(d))

    def row_part(value):
        return value[0:8], value[8:16]

    arrived(row_got_y, ("stat",))
    stats = joined([row_part(row_stat[0])] + [row_part(row_got_y[d]) for d in range(7)])
    row_stat[2, 0:8], row_stat[2, 8:16] = stats
    for d in (1, 3, 2):
        send(row_stat.at[2], row_got_x.at[d - 1], ("stat_x",), x_peer(d))
    arrived(col_got, ("stat_z",))

    def col_part(value):
        return value[0:2], value[2:4]

    top_g, total_g = joined([col_part(col_stat[...])] + [col_part(col_got[d]) for d in range(7)])
    fac = 0.5 * jnp.exp(col_stat[0:2] - top_g) / total_g
    fac_c = jnp.concatenate([upright(fac[0:1]), upright(fac[1:2])], axis=0)
    arrived(row_got_x, ("stat_x",))
    top_g, total_g = joined([stats] + [row_part(row_got_x[d]) for d in range(3)])
    fac = 0.5 * jnp.exp(row_stat[0, 0:8] - top_g) / total_g
    for q in range(4):
        for h in (0, 1):
            row = 2 * q + h
            fac_t[q, :, h * 128 : h * 128 + 128] = jnp.broadcast_to(fac[row : row + 1], (8, 128))

    number = lax.broadcasted_iota(jnp.int32, (256, 256), 0)
    clip_id = lax.shift_right_logical(number, 5) * 1024 + (number & 31) + (k * 128 + y * 32)

    def gradient(i):
        q = on_x(CHUNKS[i])
        target = jnp.concatenate([pos[0, q, 0:1, :], pos[1, q, 0:1, :]], axis=1)
        grad = exp_r[q] * fac_t[q, 0:1, :] + exp_c[q] * fac_c
        grad = grad - (clip_id == target).astype(F32)
        line = jnp.sum(grad * scores[q], axis=0, keepdims=True)
        for h in (0, 1):
            along_own[2 * i + h : 2 * i + h + 1, :] = line[:, h * 128 : h * 128 + 128]
        g_h[q], g_l[q] = split(grad * (scale * inv_t[q, 0:1, :]))
        weighted = split(grad * col_scale)
        for f in range(4):
            block = product3(weighted, (clip_h[f], clip_l[f]), ((0,), (0,)))
            part[f, q] = block.reshape(2, 128, 256)
        send(part.at[:, q, o], part_c.at[:, q], ("rc", i), partner)

    for i in range(4):
        gradient(i)
    send(along_own, along_c, ("along_c", 0), partner)

    def clip_gradient(f, carry):
        total = jnp.zeros((256, 256), F32)
        for q in range(4):
            total = total + product3((g_h[q], g_l[q]), (text_h[f, q], text_l[f, q]), ((1,), (0,)))
        cpart[:, f] = total.reshape(8, 32, 256)
        return carry

    lax.fori_loop(0, 4, clip_gradient, 0)

    def ring_sum(step):
        for f in range(4):
            for way in (0, 1):
                goal = on_z(5 - step) if way == 0 else on_z(3 + step)
                if step > 2 or (step == 2 and f // 2 == way):
                    place = cgot.at[way, step - 2, f]
                    arrived(place, ("cz", step - 1, f, way))
                    cpart[goal, f] = cpart[goal, f] + place[...]
                if step > 1 or f // 2 == way:
                    send(
                        cpart.at[goal, f], cgot.at[way, step - 1, f],
                        ("cz", step, f if step < 4 else 0, way), z_peer(1 if way == 0 else 7),
                    )

    def half_of(part):
        return pl.ds(32 * part, 32)

    def pass_a(d, way, half):
        send(
            part.at[:, on_x(d), c, rows_of(0, half)], got_a.at[way, :, half_of(half)],
            ("ra", way), x_peer(TURN[way]),
        )

    def pass_b(i, d, way, half):
        send(
            part.at[on_y(d), on_x(CHUNKS[i]), c, rows_of(1, half)], got_b.at[way, i, half_of(half)],
            ("rb", i, way), y_peer(TURN[way]),
        )

    def join_cores(i):
        q = on_x(CHUNKS[i])
        arrived(part_c.at[:, q], ("rc", i))
        for f in range(4):
            part[f, q, c] = part[f, q, c] + part_c[f, q]
        for way in (0, 1):
            if i == 0:
                send(
                    part.at[:, q, c, rows_of(0, way)], got_aa.at[way], ("raa", way), x_peer(TURN[way])
                )
            if CHUNKS[i] == TURN[way]:
                pass_a(TURN[way], way, 1 - way)
            send(
                part.at[on_y(2), q, c, rows_of(1, way)], got_bb.at[way, i], ("rbb", i, way),
                y_peer(TURN[way]),
            )
        for way in (0, 1):
            pass_b(i, TURN[way], way, 1 - way)

    def relay_a():
        for way in (0, 1):
            arrived(got_aa.at[way], ("raa", way))
            at = slice(32 * way, 32 * way + 32)
            for f in range(4):
                part[f, on_x(TURN[way]), c, at] = part[f, on_x(TURN[way]), c, at] + got_aa[way, f]
            pass_a(TURN[way], way, way)

    def relay_b(i):
        q = on_x(CHUNKS[i])
        for way in (0, 1):
            arrived(got_bb.at[way, i], ("rbb", i, way))
            at = slice(64 + 32 * way, 96 + 32 * way)
            part[on_y(TURN[way]), q, c, at] = part[on_y(TURN[way]), q, c, at] + got_bb[way, i]
            pass_b(i, TURN[way], way, way)

    def finish_a():
        for way in (0, 1):
            arrived(got_a.at[way], ("ra", way))
        for d in (2, 1, 3, 0):
            e = on_y(d)
            part[e, x, c, 0:64] = part[e, x, c, 0:64] + got_a[0, e] + got_a[1, e]
            if d > 0:
                send(part.at[e, x, c, rows_of(0)], got_ya.at[d - 1], ("ya",), y_peer(d))

    def finish_b(i):
        q = on_x(CHUNKS[i])
        for way in (0, 1):
            arrived(got_b.at[way, i], ("rb", i, way))
        part[y, q, c, 64:128] = part[y, q, c, 64:128] + got_b[0, i] + got_b[1, i]
        d = CHUNKS[i]
        if d > 0:
            send(part.at[y, q, c, rows_of(1)], got_xb.at[d - 1], ("xb",), x_peer(d))

    join_cores(0)
    ring_sum(1)
    join_cores(1)
    join_cores(2)
    join_cores(3)
    arrived(along_c, ("along_c", 0))
    along_pair[...] = along_own[...] + along_c[...]
    for d in (2, 1, 3):
        send(along_pair, along_y.at[d - 1], ("along_y",), y_peer(d))
    relay_a()
    relay_b(0)
    ring_sum(2)
    relay_b(1)
    relay_b(2)
    arrived(along_y, ("along_y",))
    along_sum[...] = along_pair[...] + along_y[0] + along_y[1] + along_y[2]
    for d in (2, 1, 3):
        send(along_sum, along_x.at[d - 1], ("along_x",), x_peer(d))
    relay_b(3)
    ring_sum(3)
    finish_b(0)
    finish_a()
    for i in (1, 2, 3):
        finish_b(i)
    ring_sum(4)

    def clip_rows():
        for way in (0, 1):
            arrived(cgot.at[way, 3], ("cz", 4, 0, way))
        squares = jnp.zeros((32, 1), F32)
        along = jnp.zeros((32, 1), F32)
        for f in range(4):
            total = cpart[z, f] + cgot[0, 3, f] + cgot[1, 3, f]
            raw = clip[z, f]
            cback[f] = total
            squares = squares + jnp.sum(raw * raw, axis=1, keepdims=True)
            along = along + jnp.sum(raw * total, axis=1, keepdims=True)
        inverse = lax.rsqrt(squares + EPSILON)
        for f in range(4):
            cback[f] = (cback[f] - (clip[z, f] * inverse) * (along * inverse)) * inverse
        for d in (1, 3, 2):
            send(cback.at[on_y(d)], col_keep.at[d - 1], ("gc",), y_peer(d))

    squares = jnp.zeros((128, 1), F32)
    for f in range(4):
        raw = text[f, x, c]
        squares = squares + jnp.sum(raw * raw, axis=1, keepdims=True)
    inverse = lax.rsqrt(squares + EPSILON)
    arrived(got_ya, ("ya",))
    arrived(got_xb, ("xb",))
    arrived(along_x, ("along_x",))
    lines = along_sum[6:8]
    for d in (1, 2, 3):
        at = 2 * CHUNKS.index(d)
        lines = lines + along_x[d - 1, at : at + 2]
    along = upright(jnp.where(c == 0, lines[0:1], lines[1:2]))
    upper = part[y, x, c, 0:64] + got_ya[0] + got_ya[1] + got_ya[2]
    lower = part[y, x, c, 64:128] + got_xb[0] + got_xb[1] + got_xb[2]
    cot = jnp.concatenate([upper, lower], axis=0)
    back = (cot - (text[y, x, c] * inverse) * along) * inverse

    order = (4, 3, 5, 2, 6, 1, 7, 0)
    back_parts = split(back)

    def weight(t):
        for j in range(4 * t, 4 * t + 4):
            rows = pl.ds(pl.multiple_of(on_z(order[j]) * 128, 128), 128)
            block = product3((hid_h[:, rows], hid_l[:, rows]), back_parts, ((0,), (0,)))
            wpart[j] = block.reshape(4, 2, 16, 256)
        send(wpart.at[4 * t : 4 * t + 4, :, o], wgot_c.at[4 * t : 4 * t + 4], ("wc", t), partner)

    def hidden(d):
        rows = pl.ds(pl.multiple_of(on_y(d) * 256, 256), 256)
        hpart[d] = product3(back_parts, (w_h[rows, :], w_l[rows, :]), ((1,), (1,)))
        if d > 0:
            send(hpart.at[d], hgot.at[d - 1], ("hid",), y_peer(d))

    def weight_x(t):
        arrived(wgot_c.at[4 * t : 4 * t + 4], ("wc", t))
        for j in range(4 * t, 4 * t + 4):
            for f in range(4):
                wpart[j, f, c] = wpart[j, f, c] + wgot_c[j, f]
        for d in (2, 1, 3):
            send(
                wpart.at[4 * t : 4 * t + 4, on_x(d), c], wgot_x.at[d - 1, 4 * t : 4 * t + 4],
                ("wx", t), x_peer(d),
            )

    def weight_z(t):
        arrived(wgot_x.at[:, 4 * t : 4 * t + 4], ("wx", t))
        for j in range(4 * t, 4 * t + 4):
            wpart[j, x, c] = wpart[j, x, c] + wgot_x[0, j] + wgot_x[1, j] + wgot_x[2, j]
            d = order[j]
            if d > 0:
                send(wpart.at[j, x, c], wgot_z.at[d - 1], ("wz",), z_peer(d))

    weight(0)
    hidden(2)
    weight(1)
    weight_x(0)
    hidden(1)
    hidden(3)
    weight_x(1)
    clip_rows()
    hidden(0)
    weight_z(0)
    gc_ref[pl.ds(pl.multiple_of(y * 32, 32), 32), :] = cback[y]
    arrived(col_keep, ("gc",))
    for d in (1, 2, 3):
        gc_ref[pl.ds(pl.multiple_of(on_y(4 - d) * 32, 32), 32), :] = col_keep[d - 1]
    weight_z(1)
    arrived(hgot, ("hid",))
    gh_ref[...] = hpart[0] + hgot[0] + hgot[1] + hgot[2]
    total = wpart[7, x, c]
    arrived(wgot_z, ("wz",))
    for d in order[:7]:
        total = total + wgot_z[d - 1]
    gw_ref[...] = total
    for group, tiles in enumerate(groups):
        whole = blank.at[pl.ds(0, tiles)]
        pltpu.make_async_remote_copy(
            src_ref=whole, dst_ref=whole, send_sem=ss.at[group], recv_sem=rs.at[0],
            device_id=partner, device_id_type=MESH,
        ).wait_send()


def body(text_hidden, proj_weight, clip_embed, positive, logit_scale):
    whole = pl.BlockSpec(memory_space=pl.ANY)
    vmem = pl.BlockSpec(memory_space=pltpu.VMEM)
    scratch = [
        ((4, 4, 2, 128, 256), F32), ((4, 4, 256, 256), BF16), ((4, 4, 256, 256), BF16),
        ((8, 4, 32, 256), F32), ((4, 256, 256), BF16), ((4, 256, 256), BF16),
        ((2, 4, 8, 128), jnp.int32), ((4, 8, 256), F32),
        ((4, 256, 256), F32), ((4, 256, 256), F32), ((4, 256, 256), F32), ((4, 8, 256), F32), ((4, 8, 256), F32),
        ((3, 16, 128), F32), ((7, 16, 128), F32), ((3, 16, 128), F32),
        ((8, 128), F32), ((7, 8, 128), F32), ((3, 32, 256), F32), ((4, 8, 256), F32),
        ((4, 256, 256), BF16), ((4, 256, 256), BF16),
        ((4, 4, 2, 128, 256), F32), ((4, 4, 128, 256), F32),
        ((2, 4, 32, 256), F32), ((2, 4, 32, 256), F32), ((2, 4, 64, 256), F32), ((2, 4, 64, 256), F32),
        ((3, 64, 256), F32), ((3, 64, 256), F32),
        ((8, 128), F32), ((8, 128), F32), ((8, 128), F32), ((3, 8, 128), F32), ((8, 128), F32), ((3, 8, 128), F32),
        ((8, 4, 32, 256), F32), ((2, 4, 4, 32, 256), F32),
        ((4, 128, 256), F32), ((3, 128, 256), F32),
        ((8, 4, 2, 16, 256), F32), ((8, 4, 16, 256), F32), ((3, 8, 16, 256), F32), ((7, 16, 256), F32),
        ((4, 32, 256), F32), ((128, 1024), F32), ((1024, 256), F32),
        ((128, 1024), BF16), ((128, 1024), BF16), ((1024, 256), BF16), ((1024, 256), BF16), ((GROUP_TILES, 8, 128), F32),
    ]
    return pl.pallas_call(
        kernel,
        out_shape=(
            pltpu.VMEM((128, 256), F32),
            pltpu.VMEM((16, 256), F32),
            pltpu.VMEM((128, 256), F32),
        ),
        in_specs=[whole, whole, vmem, vmem, pl.BlockSpec(memory_space=pltpu.SMEM)],
        out_specs=(vmem, vmem, vmem),
        scratch_shapes=[pltpu.VMEM(shape, dtype) for shape, dtype in scratch]
        + [pltpu.SemaphoreType.DMA((n,)) for n in (GROUPS, COUNT, 2)],
        compiler_params=pltpu.CompilerParams(
            collective_id=0, has_side_effects=True, vmem_limit_bytes=56 << 20
        ),
        name="contrastive",
    )(text_hidden, proj_weight, clip_embed, positive.reshape(1, 128), logit_scale)


def solution(mesh):
    rows = ("txt", "clip")
    in_specs = (P(rows, None), P(None, "proj"), P(rows, "proj"), P(rows), P())
    out_specs = (P(rows, "proj"), P(rows, "proj"), P(rows, "proj"))
    return jax.shard_map(body, mesh=mesh, in_specs=in_specs, out_specs=out_specs, check_vma=False)
```
